32 devices in a mesh: seq: 8 (over z, y), fsdp: 4 (over x, core).
Axes of the slice: x: 2, y: 2, z: 4, core: 2. Of those that a mesh axis runs over, the one named last changes fastest.
Arguments:
- inputs: bfloat16 [4, 1024, 3584], P('fsdp', 'seq'), may hold values from -36 to 36
- keys_queries: bfloat16 [4, 1024, 256], P('fsdp', 'seq'), may hold values from -0.29882812 to 0.29882812
- log_decay: float32 [4, 56, 1024], P('fsdp', None, 'seq'), may hold values from -1.5 to 0, as said below
- skip: float32 [56], replicated, may hold values from 0.5 to 1.5
- classifier: bfloat16 [3584, 128], P('fsdp'), may hold values from -0.09375 to 0.09375
Outputs:
- mixed: bfloat16 [4, 1024, 3584], P('fsdp', 'seq')
- logits: float32 [4, 128], P('fsdp')
The draws below stay inside these ranges and needn't reach their ends.
Inputs may be any that keep to these rules, and one draw needn't show every extreme that they name: `log_decay`: log-decays are negative.
All inputs are finite; a program needn't handle non-finite values.
Results may differ from the reference program's by a relative error of at most 0.0051.
Values may be sent and summed in bfloat16 or wider, within the bound.
No kernel may reach another device: no remote copies, remote signals or barrier semaphores. Data moves between devices by JAX's collectives and lax.ppermute only.
A program may use at most 256 MiB of HBM per device.

```python
import math
import jax
import jax.numpy as jnp
from jax import lax

H = 56
N = 128
K = 128
GROUP = 128
TOK_DEV = 128
HP = 3584
COPIES = 4
LEN = 1024


def draw_inputs(key, part):
    first, second, third = jax.random.split(key, 3)
    shape = (COPIES, LEN, HP)
    row_scale = jnp.exp(jax.random.uniform(second, (COPIES, LEN, 1), jnp.float32, math.log(0.3), math.log(3.0)))
    column_scale = jnp.exp(jax.random.uniform(third, (1, 1, HP), jnp.float32, math.log(0.3), math.log(3.0)))
    base = jnp.clip(jax.random.normal(first, shape, jnp.float32), -4.0, 4.0)
    return (base * row_scale * column_scale).astype(jnp.bfloat16)


def draw_log_decay(key, part):
    pieces = jax.random.split(key, 7)
    share_fast = 0.5
    chooser = jax.random.uniform(pieces[0], (COPIES, H, 1), jnp.float32)
    fast_rate = jax.random.uniform(pieces[1], (COPIES, H, 1), jnp.float32, 1.0 / 50.0, 1.0 / 30.0)
    slow_rate = jax.random.uniform(pieces[2], (COPIES, H, 1), jnp.float32, 0.05, 0.25) / LEN
    default_fading_speed = jnp.where(chooser < share_fast, fast_rate, slow_rate)
    block_count = LEN // TOK_DEV
    segment_fading_multiplier = jnp.exp(jax.random.uniform(pieces[3], (COPIES, H, block_count, 1), jnp.float32, math.log(0.5), math.log(2.0)))
    segment_fading_multiplier = jnp.broadcast_to(segment_fading_multiplier, (COPIES, H, block_count, TOK_DEV)).reshape(COPIES, H, LEN)
    offset_fading_multiplier = jnp.exp(jax.random.uniform(pieces[4], (COPIES, H, LEN), jnp.float32, math.log(0.5), math.log(2.0)))
    places = jax.random.randint(pieces[5], (COPIES, 3, 1), 0, LEN)
    damaged_symbols = (jnp.arange(LEN)[None, None, :] == places).astype(jnp.float32)
    objective_entries = jnp.log(jax.random.uniform(pieces[6], (COPIES, H, 3), jnp.float32, 0.65, 0.8))
    random_spikes = jnp.sum(damaged_symbols[:, None, :, :] * objective_entries[:, :, :, None], axis=2)
    return -default_fading_speed * segment_fading_multiplier * offset_fading_multiplier + random_spikes


def levels(rng, extent, shards, low, top_value):
    gain, own = 1.0, jax.random.fold_in(rng, 6)
    for axis_at, blocks in shards:
        heights = jnp.exp(jax.random.uniform(jax.random.fold_in(own, axis_at), (blocks,), jnp.float32, low / len(shards), top_value / len(shards)))
        gain = gain * jnp.repeat(heights, extent[axis_at] // blocks).reshape([-1 if axis == axis_at else 1 for axis in range(len(extent))])
    return gain


def centred(own_key, shape, spread, most, shards=(), kind=jnp.bfloat16):
    array = spread * jax.random.normal(own_key, shape, jnp.float32)
    if shards:
        array = array * levels(own_key, shape, shards, -0.22, 0.18)
    return jnp.clip(array, -most, most).astype(kind)


def setup_inputs(seed: int = 0) -> dict:
    seeds = jax.random.split(jax.random.key(seed), 6)
    inputs = draw_inputs(jax.random.fold_in(seeds[5], 71), 0)
    keys_queries = centred(seeds[1], (COPIES, LEN, 2 * N), 0.05, 0.29882812, ((0, 4), (1, 8)))
    log_decay = draw_log_decay(jax.random.fold_in(seeds[5], 71), 0)
    skip = jnp.clip(jax.random.uniform(seeds[3], (H,), jnp.float32, 0.5, 1.5), 0.5, 1.5)
    classifier = centred(seeds[4], (HP, K), HP ** -0.5, 0.09375, ((0, 4),))
    return dict(inputs=inputs, keys_queries=keys_queries, log_decay=log_decay, skip=skip, classifier=classifier)


epsilon = 1e-06

def reference(inputs, keys_queries, log_decay, skip, classifier):
    copies, positions, channels = inputs.shape
    head_count = log_decay.shape[1]
    head_dim = channels // head_count
    blocks = positions // GROUP
    causal = jnp.arange(GROUP)[:, None] >= jnp.arange(GROUP)[None, :]

    def group_step(carry, block_index):
        carry_state, pooled_sum = carry
        leading_row = (block_index * GROUP).astype(jnp.int32)
        value_block = lax.dynamic_slice_in_dim(inputs, leading_row, GROUP, 1)
        paired_block_matrix = lax.dynamic_slice_in_dim(keys_queries, leading_row, GROUP, 1)
        decay_block = lax.dynamic_slice_in_dim(log_decay, leading_row, GROUP, 2)
        keys = paired_block_matrix[:, :, :N].astype(jnp.float32)
        queries = paired_block_matrix[:, :, N:].astype(jnp.float32)
        values = value_block.reshape(copies, GROUP, head_count, head_dim).astype(jnp.float32)
        cumulative = jnp.cumsum(decay_block, axis=-1)
        scores = jnp.einsum('ctn,cun->ctu', queries, keys)
        decay_gap = jnp.where(causal, cumulative[:, :, :, None] - cumulative[:, :, None, :], -jnp.inf)
        mixing = (scores[:, None] * jnp.exp(decay_gap)).astype(jnp.bfloat16)
        mixing = lax.optimization_barrier(mixing).astype(jnp.float32)
        diagonal = jnp.einsum('chtu,cuhp->cthp', mixing, values)
        carried = lax.optimization_barrier(carry_state.astype(jnp.bfloat16)).astype(jnp.float32)
        growth = jnp.exp(cumulative).transpose(0, 2, 1)[..., None]
        carried_out = jnp.einsum('ctn,chnp->cthp', queries, carried) * growth
        result = diagonal + carried_out + skip[None, None, :, None] * values
        final_log = cumulative[:, :, -1:]
        weighted = (keys[:, None] * jnp.exp(final_log - cumulative)[..., None]).astype(jnp.bfloat16)
        weighted = lax.optimization_barrier(weighted).astype(jnp.float32)
        block_state = jnp.einsum('chun,cuhp->chnp', weighted, values)
        carry_state = jnp.exp(final_log)[..., None] * carry_state + block_state
        pooled_sum = pooled_sum + lax.optimization_barrier(jnp.sum(result, axis=1)).reshape(copies, channels)
        return ((carry_state, pooled_sum), result.reshape(copies, GROUP, channels).astype(jnp.bfloat16))
    initial = (jnp.zeros((copies, head_count, N, head_dim), jnp.float32), jnp.zeros((copies, channels), jnp.float32))
    (final_state, pooled_sum), outputs = lax.scan(group_step, initial, jnp.arange(blocks, dtype=jnp.int32))
    mixed = outputs.transpose(1, 0, 2, 3).reshape(copies, positions, channels)
    pooled = pooled_sum / positions
    normed = (pooled / jnp.sqrt(lax.optimization_barrier(jnp.mean(pooled * pooled, axis=-1, keepdims=True)) + epsilon)).astype(jnp.bfloat16)
    logits = jnp.dot(normed, classifier, preferred_element_type=jnp.float32)
    return (mixed, logits)
```

```python
import functools
import jax
import jax.numpy as jnp
from jax import lax
from jax.experimental import pallas as pl
from jax.experimental.pallas import tpu as pltpu
from jax.sharding import PartitionSpec as P

N = 128
GROUP = 128
AUX = 16

epsilon = 1e-06

F32 = jnp.float32
BF16 = jnp.bfloat16
HIGHEST = lax.Precision.HIGHEST
LIMIT = 48 * 1024 * 1024

VMEM = pl.BlockSpec(memory_space=pltpu.VMEM)
SMEM = pl.BlockSpec(memory_space=pltpu.SMEM)


def dot(a, b, contract=((1,), (0,)), precision=None):
    return lax.dot_general(a, b, (contract, ((), ())), preferred_element_type=F32, precision=precision)


def iota(shape, dim):
    return lax.broadcasted_iota(jnp.int32, shape, dim)


def split(x):
    high = x.astype(BF16)
    return high, (x - high.astype(F32)).astype(BF16)


def cumulative_by_position(log_decay):
    upto = (iota((GROUP, GROUP), 1) <= iota((GROUP, GROUP), 0)).astype(F32)
    return dot(upto, log_decay, ((1,), (1,)), HIGHEST)


def cumulative_by_head(log_decay):
    upto = (iota((GROUP, GROUP), 0) <= iota((GROUP, GROUP), 1)).astype(F32)
    return dot(log_decay, upto, precision=HIGHEST)


def spread(x, first_head, lanes, head_dim):
    heads = x.shape[1]
    member = (iota((heads, lanes), 0) == first_head + iota((heads, lanes), 1) // head_dim).astype(BF16)
    high, low = split(x)
    return dot(high, member) + dot(low, member)


def state_kernel(head_dim, place, kq, values, log_decay, *parts):
    lanes = parts[0].shape[1]
    part_heads = lanes // head_dim
    ld = log_decay[...]
    by_position = cumulative_by_position(ld)
    decay_left = jnp.exp(by_position[GROUP - 1 :, :] - by_position)
    by_head = cumulative_by_head(ld)
    block_decay = jnp.exp(jnp.broadcast_to(by_head[:, GROUP - 1 :], by_head.shape))
    keys = jnp.transpose(kq[:, :N])
    for m, part in enumerate(parts):
        owner = place[0] ^ m
        start = pl.multiple_of(owner * lanes, 128)
        wide = spread(decay_left, owner * part_heads, lanes, head_dim)
        weighted = (values[:, pl.ds(start, lanes)].astype(F32) * wide).astype(BF16)
        part[pl.ds(0, N), :] = dot(keys, weighted).astype(BF16)
        chooser = (iota((AUX, ld.shape[0]), 1) == owner * part_heads + iota((AUX, ld.shape[0]), 0)).astype(F32)
        mine = dot(chooser, block_decay, precision=HIGHEST)
        high, low = split(mine)
        part[pl.ds(N, AUX), pl.ds(0, 128)] = high
        part[pl.ds(N, AUX), pl.ds(128, 128)] = low
        part[pl.ds(N, AUX), pl.ds(256, lanes - 256)] = jnp.zeros((AUX, lanes - 256), BF16)


def gather_parts(place, parts, ordered):
    for m, part in enumerate(parts):
        ordered[place[0] ^ m] = part[...]


def part_decay(block, lanes, head_dim):
    aux = block[N:, :]
    factor = aux[:, :128].astype(F32) + aux[:, 128:256].astype(F32)
    per = 128 // head_dim
    pieces = []
    lane = iota((1, 128), 1) // head_dim
    for i in range(lanes // 128):
        piece = factor[i * per : i * per + 1]
        for j in range(1, per):
            piece = jnp.where(lane == j, factor[i * per + j : i * per + j + 1], piece)
        pieces.append(piece)
    return jnp.concatenate(pieces, axis=1)


def total_kernel(head_dim, place, *refs):
    *parts, total, decay, ordered = refs
    lanes = total.shape[1]
    gather_parts(place, parts, ordered)
    running = ordered[0][:N].astype(F32)
    factor = part_decay(ordered[0], lanes, head_dim)
    for j in range(1, len(parts)):
        here = part_decay(ordered[j], lanes, head_dim)
        running = here * running + ordered[j][:N].astype(F32)
        factor = factor * here
    total[...] = running.astype(BF16)
    decay[...] = factor


def starts_kernel(head_dim, place, before, *refs):
    count = (len(refs) - 2) // 2
    parts, outs, ordered, results = refs[:count], refs[count : 2 * count], refs[-2], refs[-1]
    lanes = before.shape[1]
    gather_parts(place, parts, ordered)
    running = before[...].astype(F32)
    for j in range(count):
        results[j] = running.astype(BF16)
        if j < count - 1:
            running = part_decay(ordered[j], lanes, head_dim) * running + ordered[j][:N].astype(F32)
    for m, out in enumerate(outs):
        out[...] = results[place[0] ^ m]


def block_kernel(head_dim, kq, values, log_decay, skip, out):
    ld = log_decay[...]
    by_position = cumulative_by_position(ld)
    by_head = cumulative_by_head(ld)
    scores = dot(kq[:, N:], kq[:, :N], ((1,), (1,)))
    causal = iota((GROUP, GROUP), 0) >= iota((GROUP, GROUP), 1)
    per = 128 // head_dim
    lane = iota((GROUP, 128), 1) // head_dim
    lane_row = iota((1, 128), 1) // head_dim
    for i in range(values.shape[1] // 128):
        value = values[:, i * 128 : (i + 1) * 128]
        mixes, tops = [], []
        direct = jnp.zeros((1, 128), F32)
        for j in range(per):
            h = i * per + j
            gap = by_position[:, h : h + 1] - by_head[h : h + 1, :]
            mixes.append((scores * jnp.exp(jnp.where(causal, gap, -jnp.inf))).astype(BF16))
            tops.append(jnp.where(lane == j, value, jnp.zeros_like(value)))
            direct = jnp.where(lane_row == j, skip[h], direct)
        mixed = dot(jnp.concatenate(mixes, axis=1), jnp.concatenate(tops, axis=0))
        out[:, i * 128 : (i + 1) * 128] = mixed + direct * value.astype(F32)


def output_kernel(head_dim, place, kq, log_decay, local, *refs):
    *carried, mixed, pooled = refs
    lanes = carried[0].shape[1]
    part_heads = lanes // head_dim
    growth = jnp.exp(cumulative_by_position(log_decay[...]))
    queries = kq[:, N:]
    for m, state in enumerate(carried):
        owner = place[0] ^ m
        at = pl.ds(pl.multiple_of(owner * lanes, 128), lanes)
        wide = spread(growth, owner * part_heads, lanes, head_dim)
        full = local[:, at] + wide * dot(queries, state[...])
        mixed[:, at] = full.astype(BF16)
        pooled[:, at] = jnp.sum(full, axis=0, keepdims=True)


def call(kernel, outs, in_specs, scratch=(), flops=0, moved=0):
    return pl.pallas_call(
        kernel,
        out_shape=outs,
        in_specs=in_specs,
        out_specs=jax.tree.map(lambda _: VMEM, outs),
        scratch_shapes=scratch,
        cost_estimate=pl.CostEstimate(flops=flops, bytes_accessed=moved, transcendentals=0),
        compiler_params=pltpu.CompilerParams(vmem_limit_bytes=LIMIT),
    )


def local(inputs, keys_queries, log_decay, skip, classifier):
    _, positions, channels = inputs.shape
    heads = log_decay.shape[1]
    head_dim = channels // heads
    size = lax.axis_size("seq")
    group = 4
    lanes = channels // group
    index = lax.axis_index("seq")
    place = (index % group).astype(jnp.int32).reshape(1)
    values, kq, ld = inputs[0], keys_queries[0], log_decay[0]
    part = jax.ShapeDtypeStruct((N + AUX, lanes), BF16)
    state = jax.ShapeDtypeStruct((N, lanes), BF16)

    def swap(x, m):
        return lax.ppermute(x, "seq", [(i, i ^ m) for i in range(size)])

    def shift(x, by):
        return lax.ppermute(x, "seq", [(i, i + by) for i in range(size - by)])

    parts = call(
        functools.partial(state_kernel, head_dim),
        [part] * group,
        [SMEM] + [VMEM] * 3,
        flops=2 * positions * N * channels,
        moved=4 * positions * channels,
    )(place, kq, values, ld)
    parts = [parts[0]] + [swap(parts[m], m) for m in range(1, group)]

    from_block = call(
        functools.partial(block_kernel, head_dim),
        jax.ShapeDtypeStruct((positions, channels), F32),
        [VMEM] * 3 + [SMEM],
        flops=8 * positions * N * channels,
        moved=6 * positions * channels,
    )(kq, values, ld, skip)
    gathered = lax.all_gather(classifier, "fsdp", axis=0, tiled=True)

    total, decay = call(
        functools.partial(total_kernel, head_dim),
        [state, jax.ShapeDtypeStruct((1, lanes), F32)],
        [SMEM] + [VMEM] * group,
        [pltpu.VMEM((group, N + AUX, lanes), BF16)],
    )(place, *parts)
    before = shift(total, group)
    if size > 2 * group:
        before, decay = before.astype(F32), shift(decay, group)
        reach = 1
        while reach < size // group - 1:
            before = before + decay * shift(before, group * reach)
            decay = decay * shift(decay, group * reach)
            reach *= 2
        before = before.astype(BF16)
    starts = call(
        functools.partial(starts_kernel, head_dim),
        [state] * group,
        [SMEM] + [VMEM] * (group + 1),
        [pltpu.VMEM((group, N + AUX, lanes), BF16), pltpu.VMEM((group, N, lanes), BF16)],
    )(place, before, *parts)
    starts = [starts[0]] + [swap(starts[m], m) for m in range(1, group)]
    mixed, pooled = call(
        functools.partial(output_kernel, head_dim),
        [jax.ShapeDtypeStruct((positions, channels), BF16), jax.ShapeDtypeStruct((1, channels), F32)],
        [SMEM] + [VMEM] * (3 + group),
    )(place, kq, ld, from_block, *starts)

    reach = 1
    while reach < size:
        pooled = pooled + swap(pooled, reach)
        reach *= 2
    pooled = pooled / (positions * size)
    normed = (pooled / jnp.sqrt(jnp.mean(pooled * pooled, axis=-1, keepdims=True) + epsilon)).astype(BF16)
    logits = jnp.dot(normed, gathered, preferred_element_type=F32)
    return mixed[None], logits


def solution(mesh):
    return jax.shard_map(
        local,
        mesh=mesh,
        in_specs=(
            P("fsdp", "seq", None),
            P("fsdp", "seq", None),
            P("fsdp", None, "seq"),
            P(),
            P("fsdp", None),
        ),
        out_specs=(P("fsdp", "seq", None), P("fsdp", None)),
        check_vma=False,
    )
```

```python
import functools
import jax
import jax.numpy as jnp
from jax import lax
from jax.experimental import pallas as pl
from jax.experimental.pallas import tpu as pltpu
from jax.sharding import PartitionSpec as P

N = 128
GROUP = 128

epsilon = 1e-06

F32 = jnp.float32
BF16 = jnp.bfloat16
HIGHEST = lax.Precision.HIGHEST
LIMIT = 48 * 1024 * 1024

VMEM = pl.BlockSpec(memory_space=pltpu.VMEM)
HBM = pl.BlockSpec(memory_space=pltpu.HBM)
SMEM = pl.BlockSpec(memory_space=pltpu.SMEM)


def dot(a, b, contract=((1,), (0,)), precision=None):
    return lax.dot_general(a, b, (contract, ((), ())), preferred_element_type=F32, precision=precision)


def iota(shape, dim):
    return lax.broadcasted_iota(jnp.int32, shape, dim)


def split(x):
    high = x.astype(BF16)
    return high, (x - high.astype(F32)).astype(BF16)


def cumulative_by_position(log_decay):
    upto = (iota((GROUP, GROUP), 1) <= iota((GROUP, GROUP), 0)).astype(F32)
    return dot(upto, log_decay, ((1,), (1,)), HIGHEST)


def cumulative_by_head(log_decay):
    upto = (iota((GROUP, GROUP), 0) <= iota((GROUP, GROUP), 1)).astype(F32)
    return dot(log_decay, upto, precision=HIGHEST)


def spread(x, first_head, lanes, head_dim):
    heads = x.shape[1]
    member = (iota((heads, lanes), 0) == first_head + iota((heads, lanes), 1) // head_dim).astype(BF16)
    return dot(jnp.concatenate(split(x), axis=1), jnp.concatenate([member, member], axis=0))


def state_kernel(head_dim, place, kq_from, values_from, log_decay_from, *refs):
    *parts, kq, values, log_decay, sem = refs
    copies = [
        pltpu.make_async_copy(source, target, sem.at[i])
        for i, (source, target) in enumerate(
            [(log_decay_from, log_decay), (kq_from, kq), (values_from, values)]
        )
    ]
    for copy in copies:
        copy.start()
    lanes = parts[0].shape[1]
    part_heads = lanes // head_dim
    copies[0].wait()
    by_position = cumulative_by_position(log_decay[...])
    decay_left = jnp.exp(by_position[GROUP - 1 :, :] - by_position)
    copies[1].wait()
    keys = jnp.transpose(kq[:, :N])
    wides = [spread(decay_left, (place[0] ^ m) * part_heads, lanes, head_dim) for m in range(len(parts))]
    copies[2].wait()
    for m, part in enumerate(parts):
        start = pl.multiple_of((place[0] ^ m) * lanes, 128)
        weighted = (values[:, pl.ds(start, lanes)].astype(F32) * wides[m]).astype(BF16)
        part[...] = dot(keys, weighted).astype(BF16)


def note_rows(lanes, head_dim):
    sums = -(-(lanes // 128) // 8) * 8
    heads = -(-(lanes // head_dim) // 8) * 8
    return sums, heads, sums + 2 * heads


def block_kernel(head_dim, place, kq, values, log_decay, skip, out, wide_growth, *refs):
    *notes, own_sums = refs
    ld = log_decay[...]
    channels = values.shape[1]
    lanes = channels // len(notes)
    part_heads = lanes // head_dim
    by_position = cumulative_by_position(ld)
    by_head = cumulative_by_head(ld)
    queries = kq[:, N:]
    scores = dot(queries, kq[:, :N], ((1,), (1,)))
    causal = iota((GROUP, GROUP), 0) >= iota((GROUP, GROUP), 1)
    per = 128 // head_dim
    lane = iota((GROUP, 128), 1) // head_dim
    lane_row = iota((1, 128), 1) // head_dim
    sums_rows, heads_rows, _ = note_rows(lanes, head_dim)
    own_sums[...] = jnp.zeros_like(own_sums)
    for i in range(channels // 128):
        at = slice(i * 128, (i + 1) * 128)
        value = values[:, at]
        mixes, tops = [], []
        direct = jnp.zeros((1, 128), F32)
        growth = None
        for j in range(per):
            h = i * per + j
            here = jnp.broadcast_to(by_position[:, h : h + 1], (GROUP, 128))
            gap = here - by_head[h : h + 1, :]
            mixes.append((scores * jnp.exp(jnp.where(causal, gap, -jnp.inf))).astype(BF16))
            tops.append(jnp.where(lane == j, value, jnp.zeros_like(value)))
            direct = jnp.where(lane_row == j, skip[h], direct)
            growth = here if growth is None else jnp.where(lane == j, here, growth)
        mixed = dot(jnp.concatenate(mixes, axis=1), jnp.concatenate(tops, axis=0))
        mixed = mixed + direct * value.astype(F32)
        out[:, at] = mixed
        wide_growth[:, at] = jnp.exp(growth)
        part, row = divmod(i, lanes // 128)
        own_sums[part, row : row + 1, :] = jnp.sum(mixed, axis=0, keepdims=True)

    high, low = split(jnp.exp(by_head))
    grown = dot(high, queries) + dot(low, queries)
    factor = jnp.exp(jnp.broadcast_to(by_head[:, GROUP - 1 :], by_head.shape))
    both = jnp.concatenate([grown, factor], axis=1)
    for m, note in enumerate(notes):
        first = (place[0] ^ m) * part_heads
        own = (iota((heads_rows, ld.shape[0]), 1) == first + iota((heads_rows, ld.shape[0]), 0)).astype(F32)
        mine = dot(own, both, precision=HIGHEST)
        note[pl.ds(0, sums_rows), :] = own_sums[place[0] ^ m]
        note[pl.ds(sums_rows, heads_rows), :] = mine[:, :128]
        note[pl.ds(sums_rows + heads_rows, heads_rows), :] = mine[:, 128:]


def wide_factor(factor, lanes, head_dim):
    per = 128 // head_dim
    pieces = []
    lane = iota((1, 128), 1) // head_dim
    for i in range(lanes // 128):
        piece = factor[i * per : i * per + 1]
        for j in range(1, per):
            piece = jnp.where(lane == j, factor[i * per + j : i * per + j + 1], piece)
        pieces.append(piece)
    return jnp.concatenate(pieces, axis=1)


def part_decay(note, lanes, head_dim):
    sums_rows, heads_rows, rows = note_rows(lanes, head_dim)
    return wide_factor(note[sums_rows + heads_rows : rows, :], lanes, head_dim)


def gather_parts(place, parts, notes, ordered, ordered_notes):
    for m, (part, note) in enumerate(zip(parts, notes)):
        ordered[place[0] ^ m] = part[...]
        ordered_notes[place[0] ^ m] = note[...]


def total_kernel(head_dim, count, place, *refs):
    parts, notes = refs[:count], refs[count : 2 * count]
    total, *decay, ordered_notes, scales = refs[2 * count :]
    lanes = total.shape[1]
    sums_rows, heads_rows, _ = note_rows(lanes, head_dim)
    at = pl.ds(sums_rows + heads_rows, heads_rows)
    for m, note in enumerate(notes):
        ordered_notes[place[0] ^ m] = note[at, :]
    factor = jnp.ones((heads_rows, 128), F32)
    for j in reversed(range(count)):
        scales[j] = wide_factor(factor, lanes, head_dim)
        factor = factor * ordered_notes[j]
    running = scales[place[0]] * parts[0][...].astype(F32)
    for m in range(1, count):
        running = running + scales[place[0] ^ m] * parts[m][...].astype(F32)
    total[...] = running.astype(BF16)
    for out in decay:
        out[...] = wide_factor(factor, lanes, head_dim)


def starts_kernel(head_dim, count, place, before, _, *refs):
    parts, notes, outs = refs[:count], refs[count : 2 * count], refs[2 * count : 3 * count]
    ordered, ordered_notes, results = refs[3 * count :]
    lanes = before.shape[1]
    gather_parts(place, parts, notes, ordered, ordered_notes)
    running = jnp.where(place[1] == 0, 0.0, before[...].astype(F32))
    for j in range(count):
        results[j] = running.astype(BF16)
        if j < count - 1:
            running = part_decay(ordered_notes[j], lanes, head_dim) * running + ordered[j].astype(F32)
    for m, out in enumerate(outs):
        out[...] = results[place[0] ^ m]


def base_kernel(head_dim, count, place, *refs):
    parts, notes = refs[:count], refs[count : 2 * count]
    base, ordered, ordered_notes = refs[2 * count :]
    lanes = parts[0].shape[1]
    sums_rows, heads_rows, rows = note_rows(lanes, head_dim)
    gather_parts(place, parts, notes, ordered, ordered_notes)
    sums = ordered_notes[0, pl.ds(0, sums_rows), :]
    weight = ordered_notes[0, pl.ds(sums_rows, heads_rows), :]
    factor = ordered_notes[0, pl.ds(sums_rows + heads_rows, heads_rows), :]
    running = ordered[0].astype(F32)
    carried = jnp.zeros((heads_rows, lanes), F32)
    for j in range(1, count):
        query_sums = ordered_notes[j, pl.ds(sums_rows, heads_rows), :]
        sums = sums + ordered_notes[j, pl.ds(0, sums_rows), :]
        weight = weight + factor * query_sums
        factor = factor * ordered_notes[j, pl.ds(sums_rows + heads_rows, heads_rows), :]
        carried = carried + heads_dot(query_sums, running.astype(BF16))
        running = part_decay(ordered_notes[j], lanes, head_dim) * running + ordered[j].astype(F32)
    carried = own_heads(carried, head_dim)
    for i in range(lanes // 128):
        base[i : i + 1, :] = sums[i : i + 1] + carried[:, i * 128 : (i + 1) * 128]
    for i in range(lanes // 128, sums_rows):
        base[i : i + 1, :] = jnp.zeros((1, 128), F32)
    base[pl.ds(sums_rows, heads_rows), :] = weight


def heads_dot(query_sums, state):
    rows = query_sums.shape[0]
    both = dot(jnp.concatenate(split(query_sums), axis=0), state)
    return both[:rows] + both[rows:]


def own_heads(x, head_dim):
    mine = iota(x.shape, 0) == iota(x.shape, 1) // head_dim
    return jnp.sum(jnp.where(mine, x, 0.0), axis=0, keepdims=True)


def share_of(pooled, classifier, out):
    high, low = split(pooled)
    weights = classifier[...]
    out[0:1, :] = dot(high, weights) + dot(low, weights)
    out[1:2, :] = jnp.broadcast_to(jnp.sum(pooled * pooled, axis=1, keepdims=True), (1, weights.shape[1]))
    out[2:, :] = jnp.zeros((out.shape[0] - 2, weights.shape[1]), F32)


def pooled_kernel(head_dim, positions, place, mine, other, total, before, classifier, out):
    lanes = total.shape[1]
    sums_rows, heads_rows, _ = note_rows(lanes, head_dim)
    first = place[1] == 0
    at = pl.ds(sums_rows, heads_rows)
    weight = jnp.where(first, other[at, :], mine[at, :])
    state = jnp.where(first, total[...].astype(F32), before[...].astype(F32)).astype(BF16)
    carried = own_heads(heads_dot(weight, state), head_dim)
    rows = mine[pl.ds(0, sums_rows), :] + other[pl.ds(0, sums_rows), :]
    sums = carried + jnp.concatenate([rows[i : i + 1] for i in range(lanes // 128)], axis=1)
    share_of(sums / positions, classifier, out)


def sums_kernel(head_dim, count, *refs):
    notes, states, sums = refs[:count], refs[count : 2 * count], refs[-1]
    lanes = sums.shape[1]
    sums_rows, heads_rows, _ = note_rows(lanes, head_dim)
    carried = jnp.zeros((heads_rows, lanes), F32)
    for note, state in zip(notes, states):
        carried = carried + heads_dot(note[pl.ds(sums_rows, heads_rows), :], state[...])
    carried = own_heads(carried, head_dim)
    rows = notes[0][pl.ds(0, sums_rows), :]
    for note in notes[1:]:
        rows = rows + note[pl.ds(0, sums_rows), :]
    own = jnp.concatenate([rows[i : i + 1] for i in range(lanes // 128)], axis=1)
    sums[...] = carried + own


def logits_kernel(positions, sums, classifier, out):
    share_of(sums[...] / positions, classifier, out)


def scale_kernel(channels, *refs):
    *shares, _, logits = refs
    whole = shares[0][...]
    for share in shares[1:]:
        whole = whole + share[...]
    logits[...] = whole[0:1] / jnp.sqrt(whole[1:2] / channels + epsilon)


def output_kernel(ms, aliased, place, kq, local, wide_growth, *refs):
    carried, refs = refs[: len(ms)], refs[len(ms) + aliased :]
    mixed, done, made, sem = refs
    lanes = carried[0].shape[1]
    queries = kq[:, N:]
    copies = []
    for i, (m, state) in enumerate(zip(ms, carried)):
        at = pl.ds(pl.multiple_of((place[0] ^ m) * lanes, 128), lanes)
        made[i] = (local[:, at] + wide_growth[:, at] * dot(queries, state[...])).astype(BF16)
        copies.append(pltpu.make_async_copy(made.at[i], mixed.at[:, at], sem.at[i]))
        copies[-1].start()
    for copy in copies:
        copy.wait()
    done[...] = jnp.zeros_like(done)


def call(kernel, outs, in_specs, scratch=(), flops=0, moved=0, out_specs=None, aliases=None):
    return pl.pallas_call(
        kernel,
        out_shape=outs,
        in_specs=in_specs,
        out_specs=out_specs or jax.tree.map(lambda _: VMEM, outs),
        scratch_shapes=scratch,
        input_output_aliases=aliases or {},
        cost_estimate=pl.CostEstimate(flops=flops, bytes_accessed=moved, transcendentals=0),
        compiler_params=pltpu.CompilerParams(vmem_limit_bytes=LIMIT),
    )


def local(inputs, keys_queries, log_decay, skip, classifier):
    _, positions, channels = inputs.shape
    heads = log_decay.shape[1]
    head_dim = channels // heads
    size, wide = lax.axis_size("seq"), lax.axis_size("fsdp")
    group = wide
    lanes = channels // group
    index = lax.axis_index("seq")
    place = jnp.stack([index % group, index // group]).astype(jnp.int32)
    values, kq, ld = inputs[0], keys_queries[0], log_decay[0]
    state = jax.ShapeDtypeStruct((N, lanes), BF16)
    note = jax.ShapeDtypeStruct((note_rows(lanes, head_dim)[2], 128), F32)
    row = jax.ShapeDtypeStruct((1, lanes), F32)
    full = jax.ShapeDtypeStruct((positions, channels), F32)
    gathered = [pltpu.VMEM((group, *state.shape), BF16), pltpu.VMEM((group, *note.shape), F32)]

    def swap(x, m):
        return lax.ppermute(x, "seq", [(i, i ^ m) for i in range(size)])

    def swap_all(xs):
        return [xs[0]] + [swap(xs[m], m) for m in range(1, group)]

    def shift(x, by):
        return lax.ppermute(x, "seq", [(i, i + by) for i in range(size - by)])

    *parts, kq, values, ld = call(
        functools.partial(state_kernel, head_dim),
        [state] * group + [jax.ShapeDtypeStruct(x.shape, x.dtype) for x in (kq, values, ld)],
        [SMEM] + [HBM] * 3,
        [pltpu.SemaphoreType.DMA((3,))],
        flops=2 * positions * N * channels,
        moved=4 * positions * channels,
    )(place, kq, values, ld)
    parts = swap_all(parts)

    from_block, wide_growth, *notes = call(
        functools.partial(block_kernel, head_dim),
        [full, full] + [note] * group,
        [SMEM] + [VMEM] * 3 + [SMEM],
        [pltpu.VMEM((group, note_rows(lanes, head_dim)[0], 128), F32)],
        flops=8 * positions * N * channels,
        moved=6 * positions * channels,
    )(place, kq, values, ld, skip)
    notes = swap_all(notes)

    pair = size == 2 * group
    total, *decay = call(
        functools.partial(total_kernel, head_dim, group),
        [state] if pair else [state, row],
        [SMEM] + [VMEM] * (2 * group),
        [pltpu.VMEM((group, note_rows(lanes, head_dim)[1], 128), F32), pltpu.VMEM((group, *row.shape), F32)],
    )(place, *parts, *notes)
    rows, _ = lax.optimization_barrier((classifier, total))
    rows = lax.ppermute(
        rows,
        ("seq", "fsdp"),
        [((s - s % group + f) * wide + s % group, s * wide + f) for s in range(size) for f in range(wide)],
    )
    if pair:
        before = swap(total, group)
        base = call(
            functools.partial(base_kernel, head_dim, group),
            jax.ShapeDtypeStruct((sum(note_rows(lanes, head_dim)[:2]), 128), F32),
            [SMEM] + [VMEM] * (2 * group),
            gathered,
        )(place, *parts, *notes)
        other = swap(base, group)
    else:
        before, decay = shift(total, group).astype(F32), shift(decay[0], group)
        reach = 1
        while reach < size // group - 1:
            before = before + decay * shift(before, group * reach)
            decay = decay * shift(decay, group * reach)
            reach *= 2
        before = before.astype(BF16)
        other = decay
    starts = call(
        functools.partial(starts_kernel, head_dim, group),
        [state] * group,
        [SMEM] + [VMEM] * (2 * group + 2),
        [*gathered, pltpu.VMEM((group, *state.shape), BF16)],
    )(place, before, other, *parts, *notes)
    carried = swap_all(starts)

    out = jax.ShapeDtypeStruct((8, classifier.shape[1]), F32)
    if pair:
        share = call(
            functools.partial(pooled_kernel, head_dim, positions * size), out, [SMEM] + [VMEM] * 5
        )(place, base, other, total, before, rows)
    else:
        sums = call(functools.partial(sums_kernel, head_dim, group), row, [VMEM] * (2 * group))(*notes, *starts)
        reach = group
        while reach < size:
            sums = sums + swap(sums, reach)
            reach *= 2
        share = call(functools.partial(logits_kernel, positions * size), out, [VMEM] * 2)(sums, rows)
    shares = swap_all([share] * group)

    mixed = jax.ShapeDtypeStruct((positions, channels), BF16)
    for ms in (tuple(range(group - 1)), (group - 1,)):
        made = () if isinstance(mixed, jax.ShapeDtypeStruct) else (mixed,)
        mixed, done = call(
            functools.partial(output_kernel, ms, len(made)),
            [jax.ShapeDtypeStruct((positions, channels), BF16), jax.ShapeDtypeStruct((8, 128), F32)],
            [SMEM] + [VMEM] * (3 + len(ms)) + [HBM] * len(made),
            [pltpu.VMEM((len(ms), positions, lanes), BF16), pltpu.SemaphoreType.DMA((len(ms),))],
            out_specs=[HBM, VMEM],
            aliases={4 + len(ms): 0} if made else None,
        )(place, kq, from_block, wide_growth, *[carried[m] for m in ms], *made)
    logits = call(
        functools.partial(scale_kernel, channels),
        jax.ShapeDtypeStruct((1, classifier.shape[1]), F32),
        [VMEM] * (group + 1),
    )(*shares, done)
    return mixed[None], logits


def solution(mesh):
    return jax.shard_map(
        local,
        mesh=mesh,
        in_specs=(
            P("fsdp", "seq", None),
            P("fsdp", "seq", None),
            P("fsdp", None, "seq"),
            P(),
            P("fsdp", None),
        ),
        out_specs=(P("fsdp", "seq", None), P("fsdp", None)),
        check_vma=False,
    )
```

```python
import functools
import jax
import jax.numpy as jnp
from jax import lax
from jax.experimental import pallas as pl
from jax.experimental.pallas import tpu as pltpu
from jax.sharding import PartitionSpec as P

N = 128
GROUP = 128

epsilon = 1e-06
PIECES = 2

F32 = jnp.float32
BF16 = jnp.bfloat16
HIGHEST = lax.Precision.HIGHEST
LIMIT = 48 * 1024 * 1024

VMEM = pl.BlockSpec(memory_space=pltpu.VMEM)
ANY = pl.BlockSpec(memory_space=pl.ANY)
SMEM = pl.BlockSpec(memory_space=pltpu.SMEM)


def dot(a, b, contract=((1,), (0,)), precision=None):
    return lax.dot_general(a, b, (contract, ((), ())), preferred_element_type=F32, precision=precision)


def iota(shape, dim):
    return lax.broadcasted_iota(jnp.int32, shape, dim)


def split(x):
    high = x.astype(BF16)
    return high, (x - high.astype(F32)).astype(BF16)


def cumulative_by_position(log_decay):
    upto = (iota((GROUP, GROUP), 1) <= iota((GROUP, GROUP), 0)).astype(F32)
    return dot(upto, log_decay, ((1,), (1,)), HIGHEST)


def cumulative_by_head(log_decay):
    upto = (iota((GROUP, GROUP), 0) <= iota((GROUP, GROUP), 1)).astype(F32)
    return dot(log_decay, upto, precision=HIGHEST)


def spread(x, first_head, lanes, head_dim):
    heads = x.shape[1]
    member = (iota((heads, lanes), 0) == first_head + iota((heads, lanes), 1) // head_dim).astype(BF16)
    return dot(jnp.concatenate(split(x), axis=1), jnp.concatenate([member, member], axis=0))


INDEX, WHICH, OWN, HELD = range(4)


def start_all(pairs, sems):
    copies = [pltpu.make_async_copy(source, target, sems.at[i]) for i, (source, target) in enumerate(pairs)]
    for copy in copies:
        copy.start()
    return copies


def head_rows(lanes, head_dim):
    return -(-(lanes // head_dim) // 8) * 8


def tiles_of(x):
    return [x[i : i + 1, j : j + 128] for i in range(x.shape[0]) for j in range(0, x.shape[1], 128)]


def notes_rows(tiles, width):
    return -(-tiles // (width // 128) // 8) * 8


def notes(tiles, width):
    per = width // 128
    rows = notes_rows(len(tiles), width)
    tiles = tiles + [jnp.zeros((1, 128), F32)] * (rows * per - len(tiles))
    rows = [jnp.concatenate(tiles[i : i + per], axis=1) for i in range(0, len(tiles), per)]
    return jnp.concatenate(rows, axis=0).astype(BF16)


def read_notes(ref, counts):
    tiles = tiles_of(ref[pl.ds(N, ref.shape[0] - N), :].astype(F32))
    runs = []
    for count in counts:
        runs.append(tiles[:count])
        tiles = tiles[count:]
    return runs


def wide(tiles):
    return jnp.concatenate(tiles, axis=1)


def heads_of(tiles, rows):
    return jnp.concatenate(tiles + [jnp.zeros((1, 128), F32)] * (rows - len(tiles)), axis=0)


def pieces_of(x):
    return [y.astype(F32) for y in split(x)]


def part_counts(lanes, head_dim):
    return [lanes // 128] * 2 + [lanes // head_dim] * 2


def state_kernel(head_dim, place, kq_from, values_from, log_decay_from, *refs):
    *parts, kq, values, log_decay, sems = refs
    copies = start_all([(log_decay_from, log_decay), (kq_from, kq), (values_from, values)], sems)
    lanes = parts[0].shape[1]
    part_heads = lanes // head_dim
    copies[0].wait()
    ld = log_decay[...]
    heads = ld.shape[0]
    by_position = cumulative_by_position(ld)
    final = by_position[GROUP - 1 :, :]
    decay_left = jnp.exp(final - by_position)
    last = jnp.broadcast_to(jnp.exp(final), (8, heads))
    growth = split(jnp.exp(cumulative_by_head(ld)))
    copies[1].wait()
    query_sums = dot(growth[0], kq[:, N:]) + dot(growth[1], kq[:, N:])
    keys = jnp.transpose(kq[:, :N])
    wides = []
    for m, part in enumerate(parts):
        first = (place[OWN] ^ m) * part_heads
        broad = spread(jnp.concatenate([decay_left, last], axis=0), first, lanes, head_dim)
        wides.append(broad[:GROUP])
        own = iota((head_rows(lanes, head_dim), heads), 1) == first + iota((head_rows(lanes, head_dim), heads), 0)
        mine = dot(own.astype(F32), query_sums, precision=HIGHEST)
        tiles = [tile for x in pieces_of(broad[GROUP : GROUP + 1]) for tile in tiles_of(x)]
        tiles += [tile for x in pieces_of(mine[:part_heads]) for tile in tiles_of(x)]
        below = notes(tiles, lanes)
        part[pl.ds(N, below.shape[0]), :] = below
    copies[2].wait()
    for m, part in enumerate(parts):
        start = pl.multiple_of((place[OWN] ^ m) * lanes, 128)
        weighted = (values[:, pl.ds(start, lanes)].astype(F32) * wides[m]).astype(BF16)
        part[pl.ds(0, N), :] = dot(keys, weighted).astype(BF16)


def part_notes(part, head_dim):
    lanes = part.shape[1]
    high, low, query_high, query_low = read_notes(part, part_counts(lanes, head_dim))
    rows = head_rows(lanes, head_dim)
    queries = jnp.concatenate([heads_of(query_high, rows), heads_of(query_low, rows)], axis=0)
    return wide(high) + wide(low), queries


def block_kernel(head_dim, kq_from, values_from, log_decay_from, skip, out, wide_growth, sums, kept, *scratch):
    kq, values, log_decay, sems = scratch
    copies = start_all([(kq_from, kq), (values_from, values), (log_decay_from, log_decay)], sems)
    for copy in copies:
        copy.wait()
    ld = log_decay[...]
    by_position = cumulative_by_position(ld)
    by_head = cumulative_by_head(ld)
    queries = kq[:, N:]
    kept[...] = queries
    scores = dot(queries, kq[:, :N], ((1,), (1,)))
    causal = iota((GROUP, GROUP), 0) >= iota((GROUP, GROUP), 1)
    per = 128 // head_dim
    lane = iota((GROUP, 128), 1) // head_dim
    lane_row = iota((1, 128), 1) // head_dim
    tiles = values.shape[1] // 128
    part_tiles = tiles // (sums.shape[0] // 8)
    sums[...] = jnp.zeros_like(sums)
    for i in range(tiles):
        at = slice(i * 128, (i + 1) * 128)
        value = values[:, at]
        mixes, tops = [], []
        direct = jnp.zeros((1, 128), F32)
        growth = None
        for j in range(per):
            h = i * per + j
            here = jnp.broadcast_to(by_position[:, h : h + 1], (GROUP, 128))
            gap = here - by_head[h : h + 1, :]
            mixes.append((scores * jnp.exp(jnp.where(causal, gap, -jnp.inf))).astype(BF16))
            tops.append(jnp.where(lane == j, value, jnp.zeros_like(value)))
            direct = jnp.where(lane_row == j, skip[h], direct)
            growth = here if growth is None else jnp.where(lane == j, here, growth)
        mixed = dot(jnp.concatenate(mixes, axis=1), jnp.concatenate(tops, axis=0))
        mixed = mixed + direct * value.astype(F32)
        out[:, at] = mixed
        wide_growth[:, at] = jnp.exp(growth)
        line = i // part_tiles * 8 + i % part_tiles
        sums[line : line + 1, :] = jnp.sum(mixed, axis=0, keepdims=True)


def total_kernel(head_dim, count, width, place, *refs):
    parts, total, ordered, factors = refs[:count], *refs[count:]
    for m, part in enumerate(parts):
        ordered[place[INDEX] ^ m] = part[pl.ds(0, N), pl.ds(0, width)]
        factors[place[INDEX] ^ m] = part_notes(part, head_dim)[0][:, :width]
    running = ordered[0].astype(F32)
    for j in range(1, count):
        running = factors[j] * running + ordered[j].astype(F32)
    total[...] = running.astype(BF16)


def totals_kernel(head_dim, count, pair, place, sums, *refs):
    parts, refs = refs[:count], refs[count:]
    *totals, ordered, factors, queries = refs
    if not pair:
        *totals, decay = totals
    lanes = parts[0].shape[1]
    rows = head_rows(lanes, head_dim)
    for m, part in enumerate(parts):
        ordered[place[INDEX] ^ m] = part[pl.ds(0, N), :]
        factors[place[INDEX] ^ m], queries[place[INDEX] ^ m] = part_notes(part, head_dim)
    running = ordered[0].astype(F32)
    factor = factors[0]
    if pair:
        own = (iota((rows, lanes), 0) == iota((rows, lanes), 1) // head_dim).astype(F32) / head_dim
        weight = queries[0, pl.ds(0, rows), :] + queries[0, pl.ds(rows, rows), :]
        carried = jnp.zeros((rows, lanes), F32)
    for j in range(1, count):
        if pair:
            by_head = jnp.sum(own * factor, axis=1, keepdims=True)
            weight = weight + by_head * (queries[j, pl.ds(0, rows), :] + queries[j, pl.ds(rows, rows), :])
            carried = carried + heads_dot(queries[j].astype(BF16), running.astype(BF16))
        factor = factor * factors[j]
        running = factors[j] * running + ordered[j].astype(F32)
    at = lanes - sum(total.shape[1] for total in totals)
    for total in totals:
        total[pl.ds(0, N), :] = running[:, at : at + total.shape[1]].astype(BF16)
        at += total.shape[1]
    if pair:
        base = own_heads(carried, head_dim) + own_sums(place, sums, lanes)
        tiles = [tile for x in thirds(base) for tile in tiles_of(x.astype(F32))]
        tiles += [tile for x in pieces_of(weight[: lanes // head_dim]) for tile in tiles_of(x)]
        below = notes(tiles, totals[-1].shape[1])
        totals[-1][pl.ds(N, below.shape[0]), :] = below
    else:
        decay[...] = factor


def own_sums(place, sums, lanes):
    own = sums[pl.ds(pl.multiple_of(place[OWN] * 8, 8), 8), :]
    return wide([own[i : i + 1] for i in range(lanes // 128)])


def starts_kernel(head_dim, count, at, place, *refs):
    parts, outs, refs, scratch = refs[-3 - 2 * count : -3 - count], refs[-3 - count : -3], refs[: -3 - 2 * count], refs[-3:]
    ordered, factors, results = scratch
    lanes, width = parts[0].shape[1], outs[0].shape[1]
    for m, part in enumerate(parts):
        ordered[place[INDEX] ^ m] = part[pl.ds(0, N), pl.ds(at, width)]
        factors[place[INDEX] ^ m] = part_notes(part, head_dim)[0][:, at : at + width]
    running = jnp.where(place[WHICH] == 0, 0.0, refs[-1][pl.ds(0, N), :].astype(F32))
    for j in range(count):
        results[j] = running.astype(BF16)
        if j < count - 1:
            running = factors[j] * running + ordered[j].astype(F32)
    if len(refs) > 1:
        sums = sums_of(place, head_dim, lanes, refs[: len(refs) // 2], refs[len(refs) // 2 :])
        below = notes([tile for x in thirds(sums) for tile in tiles_of(x.astype(F32))], width)
    for m, out in enumerate(outs):
        out[pl.ds(0, N), :] = results[place[INDEX] ^ m]
        if len(refs) > 1:
            out[pl.ds(N, below.shape[0]), :] = below


def sums_of(place, head_dim, lanes, totals, before):
    first = place[WHICH] == 0
    rows = head_rows(lanes, head_dim)
    counts = [lanes // 128] * 3 + [lanes // head_dim] * 2
    mine, other = read_notes(totals[-1], counts), read_notes(before[-1], counts)
    weight = [
        jnp.where(first, heads_of(there, rows), heads_of(here, rows)) for here, there in zip(mine[3:], other[3:])
    ]
    state = [
        jnp.where(first, total[pl.ds(0, N), :].astype(F32), got[pl.ds(0, N), :].astype(F32)).astype(BF16)
        for total, got in zip(totals, before)
    ]
    product = heads_dot(jnp.concatenate(weight, axis=0).astype(BF16), wide(state))
    both = sum(wide(here) + wide(there) for here, there in zip(mine[:3], other[:3]))
    return own_heads(product, head_dim) + both


def thirds(x):
    high = x.astype(BF16)
    return high, *split(x - high.astype(F32))


def heads_dot(queries, state):
    both = dot(queries, state)
    rows = queries.shape[0] // 2
    return both[:rows] + both[rows:]


def own_heads(x, head_dim):
    mine = iota(x.shape, 0) == iota(x.shape, 1) // head_dim
    return jnp.sum(jnp.where(mine, x, 0.0), axis=0, keepdims=True)


def sums_kernel(head_dim, count, place, sums, *refs):
    parts, states, out = refs[:count], refs[count:-1], refs[-1]
    carried = 0.0
    for m, part in enumerate(parts):
        state = wide([x[pl.ds(0, N), :] for x in states[m::count]])
        carried = carried + heads_dot(part_notes(part, head_dim)[1].astype(BF16), state)
    out[...] = own_heads(carried, head_dim) + own_sums(place, sums, out.shape[1])


def output_kernel(ms, count, lanes, offset, step, positions, place, queries, local, wide_growth, *refs):
    carried, refs = refs[: len(ms)], refs[len(ms) :]
    *refs, made, sems = refs
    copies = []
    at = [pl.multiple_of((place[OWN] ^ m) * lanes + offset, 128) for m in ms]
    width = carried[0].shape[1]
    mixed = refs[{0: -1, 1: -2, 2: -3}[step]]
    for i, state in enumerate(carried):
        here = pl.ds(at[i], width)
        made[i] = (local[:, here] + wide_growth[:, here] * dot(queries[...], state[pl.ds(0, N), :])).astype(BF16)
        copies.append(pltpu.make_async_copy(made.at[i], mixed.at[:, here], sems.at[i]))
        copies[-1].start()
    if step:
        whole = shares_of(ms, lanes, positions, place, carried, refs[:count])
    if step == 1:
        refs[-1][...] = whole
    if step == 2:
        whole = whole + refs[count][...]
        logits, scaled = refs[-2], refs[-1]
        scaled[...] = jnp.broadcast_to(whole[0:1] / jnp.sqrt(whole[1:2] / (lanes * count) + epsilon), scaled.shape)
        copies.append(pltpu.make_async_copy(scaled.at[pl.ds(0, 1)], logits, sems.at[len(ms)]))
        copies[-1].start()
    for copy in copies:
        copy.wait()


def shares_of(ms, lanes, positions, place, carried, weights):
    whole = 0.0
    row = iota((8, weights[0].shape[1]), 0)
    for m, state in zip(ms, carried):
        pooled = sum(wide(x) for x in read_notes(state, [lanes // 128] * 3)) / positions
        high, low = split(jnp.broadcast_to(pooled, (8, lanes)))
        distance = place[HELD] ^ place[OWN] ^ m
        rows = weights[0][...]
        for k in range(1, len(weights)):
            rows = jnp.where(distance == k, weights[k][...], rows)
        product = dot(high, rows) + dot(low, rows)
        square = jnp.sum(pooled * pooled, axis=1, keepdims=True)
        whole = whole + jnp.where(row == 0, product, jnp.where(row == 1, square, 0.0))
    return whole


def call(kernel, outs, in_specs, scratch=(), flops=0, moved=0, out_specs=None, aliases=None):
    return pl.pallas_call(
        kernel,
        out_shape=outs,
        in_specs=in_specs,
        out_specs=out_specs or jax.tree.map(lambda _: VMEM, outs),
        scratch_shapes=scratch,
        input_output_aliases=aliases or {},
        cost_estimate=pl.CostEstimate(flops=flops, bytes_accessed=moved, transcendentals=0),
        compiler_params=pltpu.CompilerParams(vmem_limit_bytes=LIMIT),
    )


def local(inputs, keys_queries, log_decay, skip, classifier):
    _, positions, channels = inputs.shape
    heads = log_decay.shape[1]
    head_dim = channels // heads
    size, wide = lax.axis_size("seq"), lax.axis_size("fsdp")
    group = wide
    pair = size == 2 * group
    lanes = channels // group
    classes = classifier.shape[1]
    index, column = lax.axis_index("seq"), lax.axis_index("fsdp")
    place = jnp.stack([index % group, index // group, (index % group) ^ column, column]).astype(jnp.int32)
    values, kq, ld = inputs[0], keys_queries[0], log_decay[0]
    sources = [pltpu.with_memory_space_constraint(x, pltpu.HBM) for x in (kq, values, ld)]
    landing = [pltpu.VMEM(x.shape, x.dtype) for x in (kq, values, ld)] + [pltpu.SemaphoreType.DMA((3,))]
    part = jax.ShapeDtypeStruct((N + notes_rows(sum(part_counts(lanes, head_dim)), lanes), lanes), BF16)
    state = jax.ShapeDtypeStruct((N, lanes), BF16)
    row = jax.ShapeDtypeStruct((1, lanes), F32)
    full = jax.ShapeDtypeStruct((positions, channels), F32)
    share = jax.ShapeDtypeStruct((8, classes), F32)
    rows = head_rows(lanes, head_dim)

    def swap(x, m, axis="seq"):
        return lax.ppermute(x, axis, [(i, i ^ m) for i in range(lax.axis_size(axis))])

    def swap_all(xs, axis="seq"):
        return [xs[0]] + [swap(xs[m], m, axis) for m in range(1, group)]

    def shift(x, by):
        return lax.ppermute(x, "seq", [(i, i + by) for i in range(size - by)])

    parts = call(
        functools.partial(state_kernel, head_dim),
        [part] * group,
        [SMEM] + [ANY] * 3,
        landing,
        flops=2 * positions * N * channels,
        moved=4 * positions * channels,
    )(place, *sources)
    parts, skip, classifier = lax.optimization_barrier((parts, skip, classifier))
    parts = swap_all(parts)
    crossed = swap(classifier, 2, "fsdp")
    made = call(
        functools.partial(block_kernel, head_dim),
        [full, full, jax.ShapeDtypeStruct((8 * group, 128), F32), jax.ShapeDtypeStruct((positions, N), BF16)],
        [ANY] * 3 + [SMEM],
        landing,
        flops=8 * positions * N * channels,
        moved=6 * positions * channels,
    )(*sources, skip)
    from_block, wide_growth, sums, queries = made
    guard = lax.optimization_barrier((place, made, crossed))[0]
    reach = 1
    while reach < group:
        sums = sums + swap(sums, reach)
        reach *= 2

    tiles = lanes // 128
    widths = [(tiles + 1) // 2 * 128, tiles // 2 * 128] if PIECES == 2 else [lanes]
    offsets = [0, widths[0]][:PIECES]
    pieces = [jax.ShapeDtypeStruct((N, width), BF16) for width in widths]

    def with_notes(count):
        return [*pieces[:-1], jax.ShapeDtypeStruct((N + notes_rows(count, widths[-1]), widths[-1]), BF16)]

    totals = []
    if pair and PIECES == 2:
        totals.append(
            call(
                functools.partial(total_kernel, head_dim, group, widths[0]),
                pieces[0],
                [SMEM] + [VMEM] * group,
                [pltpu.VMEM((group, N, widths[0]), BF16), pltpu.VMEM((group, 1, widths[0]), F32)],
            )(guard, *parts)
        )
        guard = lax.optimization_barrier((place, totals))[0]
    totals += call(
        functools.partial(totals_kernel, head_dim, group, pair),
        with_notes(3 * tiles + 2 * (lanes // head_dim))[-1:] if pair else [*pieces, row],
        [SMEM] + [VMEM] * (1 + group),
        [
            pltpu.VMEM((group, *state.shape), BF16),
            pltpu.VMEM((group, *row.shape), F32),
            pltpu.VMEM((group, 2 * rows, N), F32),
        ],
    )(guard, sums, *parts)
    classifier, crossed = lax.optimization_barrier((classifier, crossed, totals))[:2]
    if pair:
        before = [swap(total, group) for total in totals]
        across = [*totals, *before]
    else:
        *totals, decay = totals
        before = []
        for total, at, width in zip(totals, offsets, widths):
            running, factor = shift(total, group).astype(F32), shift(decay[:, at : at + width], group)
            reach = 1
            while reach < size // group - 1:
                running = running + factor * shift(running, group * reach)
                factor = factor * shift(factor, group * reach)
                reach *= 2
            before.append(running.astype(BF16))
    weights = [classifier, swap(classifier, 1, "fsdp"), crossed, swap(crossed, 1, "fsdp")]

    starts = []
    for k, (width, at) in enumerate(zip(widths, offsets)):
        last = k == PIECES - 1
        operands = across if last and pair else [before[k]]
        starts.append(
            call(
                functools.partial(starts_kernel, head_dim, group, at),
                [with_notes(3 * tiles)[k] if pair else pieces[k]] * group,
                [SMEM] + [VMEM] * (len(operands) + group),
                [
                    pltpu.VMEM((group, N, width), BF16),
                    pltpu.VMEM((group, 1, width), F32),
                    pltpu.VMEM((group, N, width), BF16),
                ],
            )(place, *operands, *parts)
        )
    if not pair:
        whole = call(
            functools.partial(sums_kernel, head_dim, group), row, [SMEM] + [VMEM] * (1 + (1 + PIECES) * group)
        )(place, sums, *parts, *[x for piece in starts for x in piece])
        reach = group
        while reach < size:
            whole = whole + swap(whole, reach)
            reach *= 2
        below = notes([tile for x in thirds(whole) for tile in tiles_of(x.astype(F32))], widths[-1])
        starts[-1] = [jnp.concatenate([x, below], axis=0) for x in starts[-1]]
    starts = [swap_all(x) for x in starts]

    plan = [(tuple(range(group)), k, 0) for k in range(PIECES - 1)]
    plan += [(tuple(range(group - 1)), PIECES - 1, 1), ((group - 1,), PIECES - 1, 2)]
    mixed = shares = logits = None
    for i, (ms, k, step) in enumerate(plan):
        extra = [*weights] if step else []
        extra += [shares] if step == 2 else []
        operands = [queries, from_block, wide_growth, *[starts[k][m] for m in ms], *extra]
        outs = [pltpu.HBM((positions, channels), BF16)]
        outs += {0: [], 1: [share], 2: [pltpu.HBM((1, classes), F32)]}[step]
        scratch = [pltpu.VMEM(share.shape, F32)] if step == 2 else []
        mixed, *rest = call(
            functools.partial(output_kernel, ms, group, lanes, offsets[k], step, positions * size),
            outs,
            [SMEM] + [VMEM] * len(operands) + [ANY] * (i > 0),
            scratch
            + [
                pltpu.VMEM((len(ms), positions, widths[k]), BF16),
                pltpu.SemaphoreType.DMA((len(ms) + 1,)),
            ],
            out_specs=[ANY] + {0: [], 1: [VMEM], 2: [ANY]}[step],
            aliases={1 + len(operands): 0} if i else None,
        )(place, *operands, *([mixed] if i else []))
        if step == 1:
            (shares,) = rest
        if step == 2:
            (logits,) = rest
    return mixed[None], logits


def solution(mesh):
    return jax.shard_map(
        local,
        mesh=mesh,
        in_specs=(
            P("fsdp", "seq", None),
            P("fsdp", "seq", None),
            P("fsdp", None, "seq"),
            P(),
            P("fsdp", None),
        ),
        out_specs=(P("fsdp", "seq", None), P("fsdp", None)),
        check_vma=False,
    )
```

```python
import functools
import jax
import jax.numpy as jnp
from jax import lax
from jax.experimental import pallas as pl
from jax.experimental.pallas import tpu as pltpu
from jax.sharding import PartitionSpec as P

N = 128
GROUP = 128

epsilon = 1e-06
PIECES = 2

F32 = jnp.float32
BF16 = jnp.bfloat16
HIGHEST = lax.Precision.HIGHEST
LIMIT = 48 * 1024 * 1024

VMEM = pl.BlockSpec(memory_space=pltpu.VMEM)
ANY = pl.BlockSpec(memory_space=pl.ANY)
SMEM = pl.BlockSpec(memory_space=pltpu.SMEM)


def dot(a, b, contract=((1,), (0,)), precision=None):
    return lax.dot_general(a, b, (contract, ((), ())), preferred_element_type=F32, precision=precision)


def iota(shape, dim):
    return lax.broadcasted_iota(jnp.int32, shape, dim)


def split(x):
    high = x.astype(BF16)
    return high, (x - high.astype(F32)).astype(BF16)


def cumulative_by_position(log_decay):
    upto = (iota((GROUP, GROUP), 1) <= iota((GROUP, GROUP), 0)).astype(F32)
    return dot(upto, log_decay, ((1,), (1,)), HIGHEST)


def cumulative_by_head(log_decay):
    upto = (iota((GROUP, GROUP), 0) <= iota((GROUP, GROUP), 1)).astype(F32)
    return dot(log_decay, upto, precision=HIGHEST)


def spread(x, first_head, lanes, head_dim):
    heads = x.shape[1]
    member = (iota((heads, lanes), 0) == first_head + iota((heads, lanes), 1) // head_dim).astype(BF16)
    return dot(jnp.concatenate(split(x), axis=1), jnp.concatenate([member, member], axis=0))


INDEX, WHICH, OWN, HELD = range(4)


def start_all(pairs, sems):
    copies = [pltpu.make_async_copy(source, target, sems.at[i]) for i, (source, target) in enumerate(pairs)]
    for copy in copies:
        copy.start()
    return copies


def head_rows(lanes, head_dim):
    return -(-(lanes // head_dim) // 8) * 8


def tiles_of(x):
    return [x[i : i + 1, j : j + 128] for i in range(x.shape[0]) for j in range(0, x.shape[1], 128)]


def notes_rows(tiles, width):
    return -(-tiles // (width // 128) // 8) * 8


def notes(tiles, width):
    per = width // 128
    rows = notes_rows(len(tiles), width)
    tiles = tiles + [jnp.zeros((1, 128), F32)] * (rows * per - len(tiles))
    rows = [jnp.concatenate(tiles[i : i + per], axis=1) for i in range(0, len(tiles), per)]
    return jnp.concatenate(rows, axis=0).astype(BF16)


def read_notes(ref, counts):
    tiles = tiles_of(ref[pl.ds(N, ref.shape[0] - N), :].astype(F32))
    runs = []
    for count in counts:
        runs.append(tiles[:count])
        tiles = tiles[count:]
    return runs


def wide(tiles):
    return jnp.concatenate(tiles, axis=1)


def heads_of(tiles, rows):
    return jnp.concatenate(tiles + [jnp.zeros((1, 128), F32)] * (rows - len(tiles)), axis=0)


def pieces_of(x):
    return [y.astype(F32) for y in split(x)]


def piece_counts(width, head_dim):
    return [width // 128] * 2 + [width // head_dim] * 2


def state_kernel(head_dim, count, place, kq_from, values_from, log_decay_from, *refs):
    *outs, kq, values, log_decay, sems = refs
    copies = start_all([(log_decay_from, log_decay), (kq_from, kq), (values_from, values)], sems)
    pieces = [outs[i : i + count] for i in range(0, len(outs), count)]
    lanes = sum(piece[0].shape[1] for piece in pieces)
    copies[0].wait()
    ld = log_decay[...]
    heads = ld.shape[0]
    by_position = cumulative_by_position(ld)
    final = by_position[GROUP - 1 :, :]
    decay_left = jnp.exp(final - by_position)
    last = jnp.broadcast_to(jnp.exp(final), (8, heads))
    growth = split(jnp.exp(cumulative_by_head(ld)))
    copies[1].wait()
    query_sums = dot(growth[0], kq[:, N:]) + dot(growth[1], kq[:, N:])
    keys = jnp.transpose(kq[:, :N])
    rows = head_rows(lanes, head_dim)
    broads = []
    for m in range(count):
        first = (place[OWN] ^ m) * (lanes // head_dim)
        broad = spread(jnp.concatenate([decay_left, last], axis=0), first, lanes, head_dim)
        broads.append(broad[:GROUP])
        own = iota((rows, heads), 1) == first + iota((rows, heads), 0)
        mine = dot(own.astype(F32), query_sums, precision=HIGHEST)
        at = 0
        for piece in pieces:
            width = piece[m].shape[1]
            here = mine[at // head_dim : (at + width) // head_dim]
            tiles = [tile for x in pieces_of(broad[GROUP : GROUP + 1, at : at + width]) for tile in tiles_of(x)]
            tiles += [tile for x in pieces_of(here) for tile in tiles_of(x)]
            below = notes(tiles, width)
            piece[m][pl.ds(N, below.shape[0]), :] = below
            at += width
    copies[2].wait()
    for m in range(count):
        at = 0
        for piece in pieces:
            width = piece[m].shape[1]
            start = pl.multiple_of((place[OWN] ^ m) * lanes + at, 128)
            weighted = (values[:, pl.ds(start, width)].astype(F32) * broads[m][:, at : at + width]).astype(BF16)
            piece[m][pl.ds(0, N), :] = dot(keys, weighted).astype(BF16)
            at += width


def piece_notes(piece, head_dim):
    width = piece.shape[1]
    high, low, query_high, query_low = read_notes(piece, piece_counts(width, head_dim))
    rows = head_rows(width, head_dim)
    queries = jnp.concatenate([heads_of(query_high, rows), heads_of(query_low, rows)], axis=0)
    return wide(high) + wide(low), queries


def block_kernel(head_dim, kq_from, values_from, log_decay_from, skip, out, wide_growth, sums, kept, *scratch):
    kq, values, log_decay, sems = scratch
    copies = start_all([(kq_from, kq), (values_from, values), (log_decay_from, log_decay)], sems)
    for copy in copies:
        copy.wait()
    ld = log_decay[...]
    by_position = cumulative_by_position(ld)
    by_head = cumulative_by_head(ld)
    queries = kq[:, N:]
    kept[...] = queries
    scores = dot(queries, kq[:, :N], ((1,), (1,)))
    causal = iota((GROUP, GROUP), 0) >= iota((GROUP, GROUP), 1)
    per = 128 // head_dim
    lane = iota((GROUP, 128), 1) // head_dim
    lane_row = iota((1, 128), 1) // head_dim
    tiles = values.shape[1] // 128
    part_tiles = tiles // (sums.shape[0] // 8)
    sums[...] = jnp.zeros_like(sums)
    for i in range(tiles):
        at = slice(i * 128, (i + 1) * 128)
        value = values[:, at]
        mixes, tops = [], []
        direct = jnp.zeros((1, 128), F32)
        growth = None
        for j in range(per):
            h = i * per + j
            here = jnp.broadcast_to(by_position[:, h : h + 1], (GROUP, 128))
            gap = here - by_head[h : h + 1, :]
            mixes.append((scores * jnp.exp(jnp.where(causal, gap, -jnp.inf))).astype(BF16))
            tops.append(jnp.where(lane == j, value, jnp.zeros_like(value)))
            direct = jnp.where(lane_row == j, skip[h], direct)
            growth = here if growth is None else jnp.where(lane == j, here, growth)
        mixed = dot(jnp.concatenate(mixes, axis=1), jnp.concatenate(tops, axis=0))
        mixed = mixed + direct * value.astype(F32)
        out[:, at] = mixed
        wide_growth[:, at] = jnp.exp(growth)
        line = i // part_tiles * 8 + i % part_tiles
        sums[line : line + 1, :] = jnp.sum(mixed, axis=0, keepdims=True)


def total_kernel(head_dim, place, *refs):
    *pieces, total, ordered, factors = refs
    for m, piece in enumerate(pieces):
        ordered[place[INDEX] ^ m] = piece[pl.ds(0, N), :]
        factors[place[INDEX] ^ m] = piece_notes(piece, head_dim)[0]
    running = ordered[0].astype(F32)
    for j in range(1, len(pieces)):
        running = factors[j] * running + ordered[j].astype(F32)
    total[...] = running.astype(BF16)


def totals_kernel(head_dim, count, pair, place, sums, *refs):
    scratch = refs[-3 * PIECES :]
    parts, outs = refs[: PIECES * count], refs[PIECES * count : -3 * PIECES]
    lanes = 0
    carried, weights, totals, decays = [], [], [], []
    for k in range(PIECES):
        ordered, factors, queries = scratch[3 * k : 3 * k + 3]
        for m, piece in enumerate(parts[k * count : (k + 1) * count]):
            ordered[place[INDEX] ^ m] = piece[pl.ds(0, N), :]
            factors[place[INDEX] ^ m], queries[place[INDEX] ^ m] = piece_notes(piece, head_dim)
        width = ordered.shape[2]
        lanes += width
        rows = head_rows(width, head_dim)
        running = ordered[0].astype(F32)
        factor = factors[0]
        if pair:
            own = (iota((rows, width), 0) == iota((rows, width), 1) // head_dim).astype(F32) / head_dim
            weight = queries[0, pl.ds(0, rows), :] + queries[0, pl.ds(rows, rows), :]
            added = jnp.zeros((rows, width), F32)
        for j in range(1, count):
            if pair:
                by_head = jnp.sum(own * factor, axis=1, keepdims=True)
                weight = weight + by_head * (queries[j, pl.ds(0, rows), :] + queries[j, pl.ds(rows, rows), :])
                added = added + heads_dot(queries[j].astype(BF16), running.astype(BF16))
            factor = factor * factors[j]
            running = factors[j] * running + ordered[j].astype(F32)
        totals.append(running.astype(BF16))
        decays.append(factor)
        if pair:
            carried.append(own_heads(added, head_dim))
            weights += [tile for x in pieces_of(weight[: width // head_dim]) for tile in tiles_of(x)]
    if not pair:
        for out, x in zip(outs, [*totals, wide(decays)]):
            out[...] = x
        return
    tiles = [tile for x in thirds(wide(carried)) for tile in tiles_of(x.astype(F32))] + weights
    for x in pieces_of(sums[...]):
        tiles += sums_tiles(x, lanes)
    below = notes(tiles, outs[0].shape[1])
    outs[0][pl.ds(0, N), :] = totals[-1]
    outs[0][pl.ds(N, below.shape[0]), :] = below


def sums_tiles(sums, lanes):
    return [sums[i : i + 1] for i in range(sums.shape[0]) if i % 8 < lanes // 128]


def starts_kernel(head_dim, count, lanes, place, *refs):
    refs, pieces, outs, scratch = refs[: -3 - 2 * count], refs[-3 - 2 * count : -3 - count], refs[-3 - count : -3], refs[-3:]
    ordered, factors, results = scratch
    width = outs[0].shape[1]
    for m, piece in enumerate(pieces):
        ordered[place[INDEX] ^ m] = piece[pl.ds(0, N), :]
        factors[place[INDEX] ^ m] = piece_notes(piece, head_dim)[0]
    running = jnp.where(place[WHICH] == 0, 0.0, refs[-1][pl.ds(0, N), :].astype(F32))
    for j in range(count):
        results[j] = running.astype(BF16)
        if j < count - 1:
            running = factors[j] * running + ordered[j].astype(F32)
    if len(refs) > 1:
        sums, fellows = sums_of(place, head_dim, lanes, count, refs[: len(refs) // 2], refs[len(refs) // 2 :])
        below = notes(sums_notes(sums, fellows), width)
    for m, out in enumerate(outs):
        out[pl.ds(0, N), :] = results[place[INDEX] ^ m]
        if len(refs) > 1:
            out[pl.ds(N, below.shape[0]), :] = below


def sums_notes(sums, fellows):
    tiles = [tile for x in thirds(sums) for tile in tiles_of(x.astype(F32))]
    return tiles + [tile for x in pieces_of(fellows) for tile in tiles_of(x)]


def sums_of(place, head_dim, lanes, count, totals, before):
    first = place[WHICH] == 0
    counts = [lanes // 128] * 3
    for total in totals:
        counts += [total.shape[1] // head_dim] * 2
    counts += [count * lanes // 128] * 2
    mine, other = read_notes(totals[-1], counts), read_notes(before[-1], counts)
    products = []
    for k, (total, got) in enumerate(zip(totals, before)):
        rows = head_rows(total.shape[1], head_dim)
        weight = [
            jnp.where(first, heads_of(there, rows), heads_of(here, rows))
            for here, there in zip(mine[3 + 2 * k : 5 + 2 * k], other[3 + 2 * k : 5 + 2 * k])
        ]
        state = jnp.where(first, total[pl.ds(0, N), :].astype(F32), got[pl.ds(0, N), :].astype(F32)).astype(BF16)
        products.append(own_heads(heads_dot(jnp.concatenate(weight, axis=0).astype(BF16), state), head_dim))
    fellows = sum(wide(here) + wide(there) for here, there in zip(mine[-2:], other[-2:]))
    return wide(products) + sum(wide(here) + wide(there) for here, there in zip(mine[:3], other[:3])), fellows


def thirds(x):
    high = x.astype(BF16)
    return high, *split(x - high.astype(F32))


def heads_dot(queries, state):
    both = dot(queries, state)
    rows = queries.shape[0] // 2
    return both[:rows] + both[rows:]


def own_heads(x, head_dim):
    mine = iota(x.shape, 0) == iota(x.shape, 1) // head_dim
    return jnp.sum(jnp.where(mine, x, 0.0), axis=0, keepdims=True)


def sums_kernel(head_dim, count, *refs):
    *refs, out = refs
    pieces, states = refs[: PIECES * count], refs[PIECES * count :]
    carried = []
    for k in range(PIECES):
        added = 0.0
        for piece, state in zip(pieces[k * count : (k + 1) * count], states[k * count : (k + 1) * count]):
            added = added + heads_dot(piece_notes(piece, head_dim)[1].astype(BF16), state[pl.ds(0, N), :])
        carried.append(own_heads(added, head_dim))
    out[...] = wide(carried)


def output_kernel(ms, count, lanes, offset, step, positions, place, queries, local, wide_growth, *refs):
    carried, refs = refs[: len(ms)], refs[len(ms) :]
    *refs, made, sems = refs
    copies = []
    at = [pl.multiple_of((place[OWN] ^ m) * lanes + offset, 128) for m in ms]
    width = carried[0].shape[1]
    mixed = refs[{0: -1, 1: -3, 2: -4}[step]]
    for i, state in enumerate(carried):
        here = pl.ds(at[i], width)
        made[i] = (local[:, here] + wide_growth[:, here] * dot(queries[...], state[pl.ds(0, N), :])).astype(BF16)
        copies.append(pltpu.make_async_copy(made.at[i], mixed.at[:, here], sems.at[i]))
        copies[-1].start()
    if step == 1:
        weights, (pooled, rows) = refs[:count], refs[-2:]
        for k, x in enumerate(weights):
            rows[place[HELD] ^ place[OWN] ^ k] = x[...]
        pooled[...] = jnp.zeros_like(pooled)
    if step == 2:
        before, rows, logits, pooled, scaled = refs[0], refs[1], refs[-3], refs[-2], refs[-1]
        pooled[...] = before[...]
    if step:
        for m, state in zip(ms, carried):
            *own, high, low = read_notes(state, [lanes // 128] * 3 + [count * lanes // 128] * 2)
            pooled[m] += jnp.broadcast_to(sum(wide(x) for x in own), (8, lanes))
            for k in range(count):
                part = slice(k * (lanes // 128), (k + 1) * (lanes // 128))
                pooled[place[OWN] ^ k] += jnp.broadcast_to(wide(high[part]) + wide(low[part]), (8, lanes))
    if step == 2:
        product = square = 0.0
        for m in range(count):
            mean = pooled[m] / positions
            high, low = split(mean)
            product = product + dot(high, rows[m]) + dot(low, rows[m])
            square = square + jnp.sum(mean * mean, axis=1, keepdims=True)
        scaled[...] = product / jnp.sqrt(square / (lanes * count) + epsilon)
        copies.append(pltpu.make_async_copy(scaled.at[pl.ds(0, 1)], logits, sems.at[len(ms)]))
        copies[-1].start()
    for copy in copies:
        copy.wait()


def call(kernel, outs, in_specs, scratch=(), flops=0, moved=0, out_specs=None, aliases=None):
    return pl.pallas_call(
        kernel,
        out_shape=outs,
        in_specs=in_specs,
        out_specs=out_specs or jax.tree.map(lambda _: VMEM, outs),
        scratch_shapes=scratch,
        input_output_aliases=aliases or {},
        cost_estimate=pl.CostEstimate(flops=flops, bytes_accessed=moved, transcendentals=0),
        compiler_params=pltpu.CompilerParams(vmem_limit_bytes=LIMIT),
    )


def local(inputs, keys_queries, log_decay, skip, classifier):
    _, positions, channels = inputs.shape
    heads = log_decay.shape[1]
    head_dim = channels // heads
    size, group = lax.axis_size("seq"), lax.axis_size("fsdp")
    pair = size == 2 * group
    lanes = channels // group
    classes = classifier.shape[1]
    index, column = lax.axis_index("seq"), lax.axis_index("fsdp")
    place = jnp.stack([index % group, index // group, (index % group) ^ column, column]).astype(jnp.int32)
    values, kq, ld = inputs[0], keys_queries[0], log_decay[0]
    sources = [pltpu.with_memory_space_constraint(x, pltpu.HBM) for x in (kq, values, ld)]
    landing = [pltpu.VMEM(x.shape, x.dtype) for x in (kq, values, ld)] + [pltpu.SemaphoreType.DMA((3,))]
    tiles = lanes // 128
    widths = [(tiles + 1) // 2 * 128, tiles // 2 * 128] if PIECES == 2 else [lanes]
    offsets = [0, widths[0]][:PIECES]

    def piece(width, count):
        return jax.ShapeDtypeStruct((N + (notes_rows(count, width) if count else 0), width), BF16)

    row = jax.ShapeDtypeStruct((1, lanes), F32)
    full = jax.ShapeDtypeStruct((positions, channels), F32)
    share = jax.ShapeDtypeStruct((8, classes), F32)
    gathered = [
        jax.ShapeDtypeStruct((group, 8, lanes), F32),
        jax.ShapeDtypeStruct((group, lanes, classes), BF16),
    ]
    def swap(x, m, axis="seq"):
        return lax.ppermute(x, axis, [(i, i ^ m) for i in range(lax.axis_size(axis))])

    def swap_all(xs, axis="seq"):
        return [xs[0]] + [swap(xs[m], m, axis) for m in range(1, group)]

    def shift(x, by):
        return lax.ppermute(x, "seq", [(i, i + by) for i in range(size - by)])

    parts = call(
        functools.partial(state_kernel, head_dim, group),
        [piece(width, sum(piece_counts(width, head_dim))) for width in widths for _ in range(group)],
        [SMEM] + [ANY] * 3,
        landing,
        flops=2 * positions * N * channels,
        moved=4 * positions * channels,
    )(place, *sources)
    parts = [swap_all(parts[i : i + group]) for i in range(0, len(parts), group)]
    classifier, parts[0][1] = lax.optimization_barrier((classifier, parts[0][1]))
    totals = []
    if pair and PIECES == 2:
        totals.append(
            call(
                functools.partial(total_kernel, head_dim),
                piece(widths[0], 0),
                [SMEM] + [VMEM] * group,
                [pltpu.VMEM((group, N, widths[0]), BF16), pltpu.VMEM((group, 1, widths[0]), F32)],
            )(place, *parts[0])
        )
        skip = lax.optimization_barrier((skip, totals))[0]
    made = call(
        functools.partial(block_kernel, head_dim),
        [full, full, jax.ShapeDtypeStruct((8 * group, 128), F32), jax.ShapeDtypeStruct((positions, N), BF16)],
        [ANY] * 3 + [SMEM],
        landing,
        flops=8 * positions * N * channels,
        moved=6 * positions * channels,
    )(*sources, skip)
    from_block, wide_growth, sums, queries = made
    scratch = []
    for width in widths:
        scratch += [
            pltpu.VMEM((group, N, width), BF16),
            pltpu.VMEM((group, 1, width), F32),
            pltpu.VMEM((group, 2 * head_rows(width, head_dim), N), F32),
        ]
    totals += call(
        functools.partial(totals_kernel, head_dim, group, pair),
        [piece(widths[-1], 3 * tiles + 2 * (lanes // head_dim) + 2 * group * tiles)] if pair else [piece(w, 0) for w in widths] + [row],
        [SMEM] + [VMEM] * (1 + PIECES * group),
        scratch,
    )(place, sums, *[x for part in parts for x in part])
    crossed = swap(classifier, 2, "fsdp")
    if pair:
        before = [swap(total, group) for total in totals]
        across = [*totals, *before]
    else:
        *totals, decay = totals
        before = []
        for total, at, width in zip(totals, offsets, widths):
            running, factor = shift(total, group).astype(F32), shift(decay[:, at : at + width], group)
            reach = 1
            while reach < size // group - 1:
                running = running + factor * shift(running, group * reach)
                factor = factor * shift(factor, group * reach)
                reach *= 2
            before.append(running.astype(BF16))
    weights = [classifier, swap(classifier, 1, "fsdp"), crossed, swap(crossed, 1, "fsdp")]

    starts = []
    for k, width in enumerate(widths):
        last = k == PIECES - 1
        operands = across if last and pair else [before[k]]
        starts.append(
            call(
                functools.partial(starts_kernel, head_dim, group, lanes),
                [piece(width, 3 * tiles + 2 * group * tiles if last and pair else 0)] * group,
                [SMEM] + [VMEM] * (len(operands) + group),
                [
                    pltpu.VMEM((group, N, width), BF16),
                    pltpu.VMEM((group, 1, width), F32),
                    pltpu.VMEM((group, N, width), BF16),
                ],
            )(place, *operands, *parts[k])
        )
    if not pair:
        whole = call(
            functools.partial(sums_kernel, head_dim, group), row, [VMEM] * (2 * PIECES * group)
        )(*[x for part in parts for x in part], *[x for part in starts for x in part])
        reach = group
        while reach < size:
            whole = whole + swap(whole, reach)
            reach *= 2
        reach = 1
        while reach < size:
            sums = sums + swap(sums, reach)
            reach *= 2
        below = notes(sums_notes(whole, wide(sums_tiles(sums / group, lanes))), widths[-1])
        starts[-1] = [jnp.concatenate([x, below], axis=0) for x in starts[-1]]
    starts = [swap_all(x) for x in starts]

    plan = [(tuple(range(group)), k, 0) for k in range(PIECES - 1)]
    plan += [(tuple(range(group - 1)), PIECES - 1, 1), ((group - 1,), PIECES - 1, 2)]
    mixed, rest = None, []
    for i, (ms, k, step) in enumerate(plan):
        operands = [queries, from_block, wide_growth, *[starts[k][m] for m in ms]]
        operands += {0: [], 1: weights, 2: rest}[step]
        outs = [pltpu.HBM((positions, channels), BF16)]
        outs += {0: [], 1: gathered, 2: [pltpu.HBM((1, classes), F32)]}[step]
        scratch = [pltpu.VMEM(gathered[0].shape, F32), pltpu.VMEM(share.shape, F32)] if step == 2 else []
        mixed, *rest = call(
            functools.partial(output_kernel, ms, group, lanes, offsets[k], step, positions * size),
            outs,
            [SMEM] + [VMEM] * len(operands) + [ANY] * (i > 0),
            scratch
            + [
                pltpu.VMEM((len(ms), positions, widths[k]), BF16),
                pltpu.SemaphoreType.DMA((len(ms) + 1,)),
            ],
            out_specs=[ANY] + {0: [], 1: [VMEM] * 2, 2: [ANY]}[step],
            aliases={1 + len(operands): 0} if i else None,
        )(place, *operands, *([mixed] if i else []))
    (logits,) = rest
    return mixed[None], logits


def solution(mesh):
    return jax.shard_map(
        local,
        mesh=mesh,
        in_specs=(
            P("fsdp", "seq", None),
            P("fsdp", "seq", None),
            P("fsdp", None, "seq"),
            P(),
            P("fsdp", None),
        ),
        out_specs=(P("fsdp", "seq", None), P("fsdp", None)),
        check_vma=False,
    )
```

```python
import functools
import jax
import jax.numpy as jnp
from jax import lax
from jax.experimental import pallas as pl
from jax.experimental.pallas import tpu as pltpu
from jax.sharding import PartitionSpec as P

N = 128
GROUP = 128

epsilon = 1e-06
PIECES = 2

F32 = jnp.float32
BF16 = jnp.bfloat16
HIGHEST = lax.Precision.HIGHEST
LIMIT = 48 * 1024 * 1024

VMEM = pl.BlockSpec(memory_space=pltpu.VMEM)
ANY = pl.BlockSpec(memory_space=pl.ANY)
SMEM = pl.BlockSpec(memory_space=pltpu.SMEM)


def dot(a, b, contract=((1,), (0,)), precision=None):
    return lax.dot_general(a, b, (contract, ((), ())), preferred_element_type=F32, precision=precision)


def iota(shape, dim):
    return lax.broadcasted_iota(jnp.int32, shape, dim)


def split(x):
    high = x.astype(BF16)
    return high, (x - high.astype(F32)).astype(BF16)


def cumulative_by_position(log_decay):
    upto = (iota((GROUP, GROUP), 1) <= iota((GROUP, GROUP), 0)).astype(F32)
    return dot(upto, log_decay, ((1,), (1,)), HIGHEST)


def cumulative_by_head(log_decay):
    upto = (iota((GROUP, GROUP), 0) <= iota((GROUP, GROUP), 1)).astype(F32)
    return dot(log_decay, upto, precision=HIGHEST)


def spread(x, first_head, lanes, head_dim):
    heads = x.shape[1]
    member = (iota((heads, lanes), 0) == first_head + iota((heads, lanes), 1) // head_dim).astype(BF16)
    return dot(jnp.concatenate(split(x), axis=1), jnp.concatenate([member, member], axis=0))


INDEX, WHICH, OWN, HELD = range(4)


def start_all(pairs, sems):
    copies = [pltpu.make_async_copy(source, target, sems.at[i]) for i, (source, target) in enumerate(pairs)]
    for copy in copies:
        copy.start()
    return copies


def head_rows(lanes, head_dim):
    return -(-(lanes // head_dim) // 8) * 8


def tiles_of(x):
    return [x[i : i + 1, j : j + 128] for i in range(x.shape[0]) for j in range(0, x.shape[1], 128)]


def notes_rows(tiles, width):
    return -(-tiles // (width // 128) // 8) * 8


def notes(tiles, width):
    per = width // 128
    rows = notes_rows(len(tiles), width)
    tiles = tiles + [jnp.zeros((1, 128), F32)] * (rows * per - len(tiles))
    rows = [jnp.concatenate(tiles[i : i + per], axis=1) for i in range(0, len(tiles), per)]
    return jnp.concatenate(rows, axis=0).astype(BF16)


def read_notes(ref, counts):
    tiles = tiles_of(ref[pl.ds(N, ref.shape[0] - N), :].astype(F32))
    runs = []
    for count in counts:
        runs.append(tiles[:count])
        tiles = tiles[count:]
    return runs


def wide(tiles):
    return jnp.concatenate(tiles, axis=1)


def heads_of(tiles, rows):
    return jnp.concatenate(tiles + [jnp.zeros((1, 128), F32)] * (rows - len(tiles)), axis=0)


def pieces_of(x):
    return [y.astype(F32) for y in split(x)]


def piece_counts(width, heads):
    return [width // 128] * 2 + [heads] * 2


def first_kernel(head_dim, lanes, place, kq_from, values_from, log_decay_from, *refs):
    *pieces, kq, values, log_decay, sems = refs
    copies = start_all([(log_decay_from, log_decay), (kq_from, kq), (values_from, values)], sems)
    copies[0].wait()
    decay = decay_left(log_decay[...])
    copies[1].wait()
    keys = jnp.transpose(kq[:, :N])
    wides = [spread(decay, first_head(place, m, lanes, head_dim), pieces[0].shape[1], head_dim) for m in range(len(pieces))]
    copies[2].wait()
    for m, piece in enumerate(pieces):
        state_piece(place, m, lanes, 0, keys, values, wides[m], [], piece)


def last_kernel(head_dim, lanes, place, kq, values, log_decay, *pieces):
    width = pieces[0].shape[1]
    at = lanes - width
    ld = log_decay[...]
    heads, rows = ld.shape[0], head_rows(lanes, head_dim)
    decay = decay_left(ld)
    growth = split(jnp.exp(cumulative_by_head(ld)))
    query_sums = dot(growth[0], kq[:, N:]) + dot(growth[1], kq[:, N:])
    keys = jnp.transpose(kq[:, :N])
    for m, piece in enumerate(pieces):
        first = first_head(place, m, lanes, head_dim)
        own = iota((rows, heads), 1) == first + iota((rows, heads), 0)
        mine = dot(own.astype(F32), query_sums, precision=HIGHEST)[: lanes // head_dim]
        tiles = [tile for x in pieces_of(mine) for tile in tiles_of(x)]
        broad = spread(decay, first + at // head_dim, width, head_dim)
        state_piece(place, m, lanes, at, keys, values, broad, tiles, piece)


def first_head(place, m, lanes, head_dim):
    return (place[OWN] ^ m) * (lanes // head_dim)


def decay_left(log_decay):
    by_position = cumulative_by_position(log_decay)
    final = by_position[GROUP - 1 :, :]
    return jnp.concatenate([jnp.exp(final - by_position), jnp.broadcast_to(jnp.exp(final), (8, final.shape[1]))], axis=0)


def state_piece(place, m, lanes, at, keys, values, broad, tiles, piece):
    width = piece.shape[1]
    below = notes([tile for x in pieces_of(broad[GROUP : GROUP + 1]) for tile in tiles_of(x)] + tiles, width)
    piece[pl.ds(N, below.shape[0]), :] = below
    start = pl.multiple_of((place[OWN] ^ m) * lanes + at, 128)
    weighted = (values[:, pl.ds(start, width)].astype(F32) * broad[:GROUP]).astype(BF16)
    piece[pl.ds(0, N), :] = dot(keys, weighted).astype(BF16)


def piece_factor(piece):
    high, low = read_notes(piece, [piece.shape[1] // 128] * 2)
    return wide(high) + wide(low)


def piece_queries(piece, head_dim, widths):
    _, _, high, low = read_notes(piece, piece_counts(widths[-1], sum(widths) // head_dim))
    out, at = [], 0
    for width in widths:
        rows, end = head_rows(width, head_dim), at + width // head_dim
        out.append(jnp.concatenate([heads_of(high[at:end], rows), heads_of(low[at:end], rows)], axis=0))
        at = end
    return out


def block_kernel(head_dim, kq, values, log_decay, skip, out, wide_growth, sums):
    ld = log_decay[...]
    by_position = cumulative_by_position(ld)
    by_head = cumulative_by_head(ld)
    scores = dot(kq[:, N:], kq[:, :N], ((1,), (1,)))
    causal = iota((GROUP, GROUP), 0) >= iota((GROUP, GROUP), 1)
    per = 128 // head_dim
    lane = iota((GROUP, 128), 1) // head_dim
    lane_row = iota((1, 128), 1) // head_dim
    tiles = values.shape[1] // 128
    part_tiles = tiles // (sums.shape[0] // 8)
    sums[...] = jnp.zeros_like(sums)
    for i in range(tiles):
        at = slice(i * 128, (i + 1) * 128)
        value = values[:, at]
        mixes, tops = [], []
        direct = jnp.zeros((1, 128), F32)
        growth = None
        for j in range(per):
            h = i * per + j
            here = jnp.broadcast_to(by_position[:, h : h + 1], (GROUP, 128))
            gap = here - by_head[h : h + 1, :]
            mixes.append((scores * jnp.exp(jnp.where(causal, gap, -jnp.inf))).astype(BF16))
            tops.append(jnp.where(lane == j, value, jnp.zeros_like(value)))
            direct = jnp.where(lane_row == j, skip[h], direct)
            growth = here if growth is None else jnp.where(lane == j, here, growth)
        mixed = dot(jnp.concatenate(mixes, axis=1), jnp.concatenate(tops, axis=0))
        mixed = mixed + direct * value.astype(F32)
        out[:, at] = mixed
        wide_growth[:, at] = jnp.exp(growth)
        line = i // part_tiles * 8 + i % part_tiles
        sums[line : line + 1, :] = jnp.sum(mixed, axis=0, keepdims=True)


def at_index(place, count, body):
    for index in range(count):
        pl.when(place[INDEX] == index)(functools.partial(body, index))


def total_kernel(head_dim, place, *refs):
    *pieces, total = refs
    factors = [piece_factor(piece) for piece in pieces]

    def body(index):
        running = pieces[index][pl.ds(0, N), :].astype(F32)
        for j in range(1, len(pieces)):
            running = factors[j ^ index] * running + pieces[j ^ index][pl.ds(0, N), :].astype(F32)
        total[...] = running.astype(BF16)

    at_index(place, len(pieces), body)


def totals_kernel(head_dim, count, pair, place, sums, *refs):
    scratch = refs[-3 * PIECES :]
    parts, outs = refs[: PIECES * count], refs[PIECES * count : -3 * PIECES]
    lanes = 0
    carried, weights, totals, decays = [], [], [], []
    widths = [scratch[3 * k].shape[2] for k in range(PIECES)]
    for m, piece in enumerate(parts[-count:]):
        for k, x in enumerate(piece_queries(piece, head_dim, widths)):
            scratch[3 * k + 2][place[INDEX] ^ m] = x
    for k in range(PIECES):
        ordered, factors, queries = scratch[3 * k : 3 * k + 3]
        for m, piece in enumerate(parts[k * count : (k + 1) * count]):
            ordered[place[INDEX] ^ m] = piece[pl.ds(0, N), :]
            factors[place[INDEX] ^ m] = piece_factor(piece)
        width = ordered.shape[2]
        lanes += width
        rows = head_rows(width, head_dim)
        running = ordered[0].astype(F32)
        factor = factors[0]
        if pair:
            own = (iota((rows, width), 0) == iota((rows, width), 1) // head_dim).astype(F32) / head_dim
            weight = queries[0, pl.ds(0, rows), :] + queries[0, pl.ds(rows, rows), :]
            added = jnp.zeros((rows, width), F32)
        for j in range(1, count):
            if pair:
                by_head = jnp.sum(own * factor, axis=1, keepdims=True)
                weight = weight + by_head * (queries[j, pl.ds(0, rows), :] + queries[j, pl.ds(rows, rows), :])
                added = added + heads_dot(queries[j].astype(BF16), running.astype(BF16))
            factor = factor * factors[j]
            running = factors[j] * running + ordered[j].astype(F32)
        totals.append(running.astype(BF16))
        decays.append(factor)
        if pair:
            carried.append(own_heads(added, head_dim))
            weights += [tile for x in pieces_of(weight[: width // head_dim]) for tile in tiles_of(x)]
    if not pair:
        for out, x in zip(outs, [*totals, wide(decays)]):
            out[...] = x
        return
    known = wide(sums_tiles(sums[...], lanes)) + in_own_part(place, count, wide(carried))
    below = notes(weights + sums_notes(known), outs[0].shape[1])
    outs[0][pl.ds(0, N), :] = totals[-1]
    outs[0][pl.ds(N, below.shape[0]), :] = below


def sums_tiles(sums, lanes):
    return [sums[i : i + 1] for i in range(sums.shape[0]) if i % 8 < lanes // 128]


def in_own_part(place, count, x):
    return wide([jnp.where(place[OWN] == k, x, 0.0) for k in range(count)])


def starts_kernel(head_dim, count, lanes, place, *refs):
    refs, pieces, outs = refs[: -2 * count], refs[-2 * count : -count], refs[-count:]
    factors = [piece_factor(piece) for piece in pieces]

    def body(index):
        running = jnp.where(place[WHICH] == 0, 0.0, refs[-1][pl.ds(0, N), :].astype(F32))
        for j in range(count):
            outs[j ^ index][pl.ds(0, N), :] = running.astype(BF16)
            if j < count - 1:
                running = factors[j ^ index] * running + pieces[j ^ index][pl.ds(0, N), :].astype(F32)

    at_index(place, count, body)
    if len(refs) > 1:
        sums = sums_of(place, head_dim, lanes, count, refs[: len(refs) // 2], refs[len(refs) // 2 :])
        below = notes(sums_notes(sums), outs[0].shape[1])
        for out in outs:
            out[pl.ds(N, below.shape[0]), :] = below


def sums_notes(sums):
    return [tile for x in pieces_of(sums) for tile in tiles_of(x)]


def sums_of(place, head_dim, lanes, count, totals, before):
    first = place[WHICH] == 0
    counts = []
    for total in totals:
        counts += [total.shape[1] // head_dim] * 2
    counts += [count * lanes // 128] * 2
    mine, other = read_notes(totals[-1], counts), read_notes(before[-1], counts)
    products = []
    for k, (total, got) in enumerate(zip(totals, before)):
        rows = head_rows(total.shape[1], head_dim)
        weight = [
            jnp.where(first, heads_of(there, rows), heads_of(here, rows))
            for here, there in zip(mine[2 * k : 2 * k + 2], other[2 * k : 2 * k + 2])
        ]
        state = jnp.where(first, total[pl.ds(0, N), :].astype(F32), got[pl.ds(0, N), :].astype(F32)).astype(BF16)
        products.append(own_heads(heads_dot(jnp.concatenate(weight, axis=0).astype(BF16), state), head_dim))
    known = sum(wide(here) + wide(there) for here, there in zip(mine[-2:], other[-2:]))
    return known + in_own_part(place, count, wide(products))


def heads_dot(queries, state):
    both = dot(queries, state)
    rows = queries.shape[0] // 2
    return both[:rows] + both[rows:]


def own_heads(x, head_dim):
    mine = iota(x.shape, 0) == iota(x.shape, 1) // head_dim
    return jnp.sum(jnp.where(mine, x, 0.0), axis=0, keepdims=True)


def sums_kernel(head_dim, count, *refs):
    *refs, out = refs
    pieces, states = refs[: PIECES * count], refs[PIECES * count :]
    carried = []
    widths = [pieces[k * count].shape[1] for k in range(PIECES)]
    queries = [piece_queries(piece, head_dim, widths) for piece in pieces[-count:]]
    for k in range(PIECES):
        added = 0.0
        for query, state in zip(queries, states[k * count : (k + 1) * count]):
            added = added + heads_dot(query[k].astype(BF16), state[pl.ds(0, N), :])
        carried.append(own_heads(added, head_dim))
    out[...] = wide(carried)


def output_kernel(ms, count, lanes, offset, step, positions, place, kq, local, wide_growth, *refs):
    carried, refs = refs[: len(ms)], refs[len(ms) :]
    *refs, made, sems = refs
    copies = []
    at = [pl.multiple_of((place[OWN] ^ m) * lanes + offset, 128) for m in ms]
    width = carried[0].shape[1]
    mixed = refs[{0: -1, 1: -3, 2: -4}[step]]
    for i, state in enumerate(carried):
        here = pl.ds(at[i], width)
        made[i] = (local[:, here] + wide_growth[:, here] * dot(kq[:, N:], state[pl.ds(0, N), :])).astype(BF16)
        copies.append(pltpu.make_async_copy(made.at[i], mixed.at[:, here], sems.at[i]))
        copies[-1].start()
    if step == 1:
        weights, (pooled, rows) = refs[:count], refs[-2:]
        for k in range(count):
            rows[place[HELD] ^ place[OWN] ^ k] = weights[k][...]
        pooled[...] = jnp.zeros_like(pooled)
    if step == 2:
        before, rows, logits, pooled, scaled = refs[0], refs[1], refs[-3], refs[-2], refs[-1]
        pooled[...] = before[...]
    if step:
        for m, state in zip(ms, carried):
            high, low = read_notes(state, [count * lanes // 128] * 2)
            for k in range(count):
                part = slice(k * (lanes // 128), (k + 1) * (lanes // 128))
                pooled[place[OWN] ^ k] += jnp.broadcast_to(wide(high[part]) + wide(low[part]), (8, lanes))
    if step == 2:
        product = square = 0.0
        for m in range(count):
            mean = pooled[m] / positions
            high, low = split(mean)
            product = product + dot(high, rows[m]) + dot(low, rows[m])
            square = square + jnp.sum(mean * mean, axis=1, keepdims=True)
        scaled[...] = product / jnp.sqrt(square / (lanes * count) + epsilon)
        copies.append(pltpu.make_async_copy(scaled.at[pl.ds(0, 1)], logits, sems.at[len(ms)]))
        copies[-1].start()
    for copy in copies:
        copy.wait()


def call(kernel, outs, in_specs, scratch=(), flops=0, moved=0, out_specs=None, aliases=None):
    return pl.pallas_call(
        kernel,
        out_shape=outs,
        in_specs=in_specs,
        out_specs=out_specs or jax.tree.map(lambda _: VMEM, outs),
        scratch_shapes=scratch,
        input_output_aliases=aliases or {},
        cost_estimate=pl.CostEstimate(flops=flops, bytes_accessed=moved, transcendentals=0),
        compiler_params=pltpu.CompilerParams(vmem_limit_bytes=LIMIT),
    )


def local(inputs, keys_queries, log_decay, skip, classifier):
    _, positions, channels = inputs.shape
    heads = log_decay.shape[1]
    head_dim = channels // heads
    size, group = lax.axis_size("seq"), lax.axis_size("fsdp")
    pair = size == 2 * group
    lanes = channels // group
    classes = classifier.shape[1]
    index, column = lax.axis_index("seq"), lax.axis_index("fsdp")
    place = jnp.stack([index % group, index // group, (index % group) ^ column, column]).astype(jnp.int32)
    values, kq, ld = inputs[0], keys_queries[0], log_decay[0]
    sources = [pltpu.with_memory_space_constraint(x, pltpu.HBM) for x in (kq, values, ld)]
    landing = [jax.ShapeDtypeStruct(x.shape, x.dtype) for x in (kq, values, ld)]
    tiles = lanes // 128
    widths = [(tiles + 1) // 2 * 128, tiles // 2 * 128] if PIECES == 2 else [lanes]
    offsets = [0, widths[0]][:PIECES]

    def piece(width, count):
        return jax.ShapeDtypeStruct((N + (notes_rows(count, width) if count else 0), width), BF16)

    row = jax.ShapeDtypeStruct((1, lanes), F32)
    full = jax.ShapeDtypeStruct((positions, channels), F32)
    share = jax.ShapeDtypeStruct((8, classes), F32)
    gathered = [
        jax.ShapeDtypeStruct((group, 8, lanes), F32),
        jax.ShapeDtypeStruct((group, lanes, classes), BF16),
    ]
    def swap(x, m, axis="seq"):
        return lax.ppermute(x, axis, [(i, i ^ m) for i in range(lax.axis_size(axis))])

    def swap_all(xs, axis="seq"):
        return [xs[0]] + [swap(xs[m], m, axis) for m in range(1, group)]

    def shift(x, by):
        return lax.ppermute(x, "seq", [(i, i + by) for i in range(size - by)])

    *first, kq, values, ld = call(
        functools.partial(first_kernel, head_dim, lanes),
        [piece(widths[0], sum(piece_counts(widths[0], 0)))] * group + landing,
        [SMEM] + [ANY] * 3,
        [pltpu.SemaphoreType.DMA((3,))],
        flops=2 * positions * N * channels,
        moved=4 * positions * channels,
    )(place, *sources)
    last = call(
        functools.partial(last_kernel, head_dim, lanes),
        [piece(widths[1], sum(piece_counts(widths[1], lanes // head_dim)))] * group,
        [SMEM] + [VMEM] * 3,
    )(place, kq, values, ld)
    parts = [swap_all(first), swap_all(last)]
    classifier, parts[0][1] = lax.optimization_barrier((classifier, parts[0][1]))
    totals = []
    if pair and PIECES == 2:
        totals.append(
            call(
                functools.partial(total_kernel, head_dim),
                piece(widths[0], 0),
                [SMEM] + [VMEM] * group,
            )(place, *parts[0])
        )
        skip = lax.optimization_barrier((skip, totals))[0]
    made = call(
        functools.partial(block_kernel, head_dim),
        [full, full, jax.ShapeDtypeStruct((8 * group, 128), F32)],
        [VMEM] * 3 + [SMEM],
        flops=8 * positions * N * channels,
        moved=6 * positions * channels,
    )(kq, values, ld, skip)
    from_block, wide_growth, sums = made
    scratch = []
    for width in widths:
        scratch += [
            pltpu.VMEM((group, N, width), BF16),
            pltpu.VMEM((group, 1, width), F32),
            pltpu.VMEM((group, 2 * head_rows(width, head_dim), N), F32),
        ]
    totals += call(
        functools.partial(totals_kernel, head_dim, group, pair),
        [piece(widths[-1], 2 * (lanes // head_dim) + 2 * group * tiles)] if pair else [piece(w, 0) for w in widths] + [row],
        [SMEM] + [VMEM] * (1 + PIECES * group),
        scratch,
    )(place, sums, *[x for part in parts for x in part])
    crossed = swap(classifier, 2, "fsdp")
    if pair:
        before = [swap(total, group) for total in totals]
        across = [*totals, *before]
    else:
        *totals, decay = totals
        before = []
        for total, at, width in zip(totals, offsets, widths):
            running, factor = shift(total, group).astype(F32), shift(decay[:, at : at + width], group)
            reach = 1
            while reach < size // group - 1:
                running = running + factor * shift(running, group * reach)
                factor = factor * shift(factor, group * reach)
                reach *= 2
            before.append(running.astype(BF16))

    weights = [classifier, swap(classifier, 1, "fsdp"), crossed, swap(crossed, 1, "fsdp")]
    starts = []
    for k, width in enumerate(widths):
        last = k == PIECES - 1
        operands = across if last and pair else [before[k]]
        starts.append(
            call(
                functools.partial(starts_kernel, head_dim, group, lanes),
                [piece(width, 2 * group * tiles if last and pair else 0)] * group,
                [SMEM] + [VMEM] * (len(operands) + group),
            )(place, *operands, *parts[k])
        )
    if not pair:
        whole = call(
            functools.partial(sums_kernel, head_dim, group), row, [VMEM] * (2 * PIECES * group)
        )(*[x for part in parts for x in part], *[x for part in starts for x in part])
        reach = group
        while reach < size:
            whole = whole + swap(whole, reach)
            reach *= 2
        reach = 1
        while reach < size:
            sums = sums + swap(sums, reach)
            reach *= 2
        known = wide(sums_tiles(sums / group, lanes)) + in_own_part(place, group, whole)
        below = notes(sums_notes(known), widths[-1])
        starts[-1] = [jnp.concatenate([x, below], axis=0) for x in starts[-1]]
    starts = [swap_all(x) for x in starts]

    plan = [(tuple(range(group)), k, 0) for k in range(PIECES - 1)]
    plan += [(tuple(range(group - 1)), PIECES - 1, 1), ((group - 1,), PIECES - 1, 2)]
    mixed, rest = None, []
    for i, (ms, k, step) in enumerate(plan):
        operands = [kq, from_block, wide_growth, *[starts[k][m] for m in ms]]
        operands += {0: [], 1: weights, 2: rest}[step]
        outs = [pltpu.HBM((positions, channels), BF16)]
        outs += {0: [], 1: gathered, 2: [pltpu.HBM((1, classes), F32)]}[step]
        scratch = [pltpu.VMEM(gathered[0].shape, F32), pltpu.VMEM(share.shape, F32)] if step == 2 else []
        mixed, *rest = call(
            functools.partial(output_kernel, ms, group, lanes, offsets[k], step, positions * size),
            outs,
            [SMEM] + [VMEM] * len(operands) + [ANY] * (i > 0),
            scratch
            + [
                pltpu.VMEM((len(ms), positions, widths[k]), BF16),
                pltpu.SemaphoreType.DMA((len(ms) + 1,)),
            ],
            out_specs=[ANY] + {0: [], 1: [VMEM] * 2, 2: [ANY]}[step],
            aliases={1 + len(operands): 0} if i else None,
        )(place, *operands, *([mixed] if i else []))
    (logits,) = rest
    return mixed[None], logits


def solution(mesh):
    return jax.shard_map(
        local,
        mesh=mesh,
        in_specs=(
            P("fsdp", "seq", None),
            P("fsdp", "seq", None),
            P("fsdp", None, "seq"),
            P(),
            P("fsdp", None),
        ),
        out_specs=(P("fsdp", "seq", None), P("fsdp", None)),
        check_vma=False,
    )
```

```python
import functools
import jax
import jax.numpy as jnp
from jax import lax
from jax.experimental import pallas as pl
from jax.experimental.pallas import tpu as pltpu
from jax.sharding import PartitionSpec as P

N = 128
GROUP = 128

epsilon = 1e-06
PIECES = 2

F32 = jnp.float32
BF16 = jnp.bfloat16
HIGHEST = lax.Precision.HIGHEST
LIMIT = 48 * 1024 * 1024

VMEM = pl.BlockSpec(memory_space=pltpu.VMEM)
ANY = pl.BlockSpec(memory_space=pl.ANY)
SMEM = pl.BlockSpec(memory_space=pltpu.SMEM)


def dot(a, b, contract=((1,), (0,)), precision=None):
    return lax.dot_general(a, b, (contract, ((), ())), preferred_element_type=F32, precision=precision)


def iota(shape, dim):
    return lax.broadcasted_iota(jnp.int32, shape, dim)


def split(x):
    high = x.astype(BF16)
    return high, (x - high.astype(F32)).astype(BF16)


def cumulative_by_position(log_decay):
    upto = (iota((GROUP, GROUP), 1) <= iota((GROUP, GROUP), 0)).astype(F32)
    return dot(upto, log_decay, ((1,), (1,)), HIGHEST)


def cumulative_by_head(log_decay):
    upto = (iota((GROUP, GROUP), 0) <= iota((GROUP, GROUP), 1)).astype(F32)
    return dot(log_decay, upto, precision=HIGHEST)


def spread(x, first_head, lanes, head_dim):
    heads = x.shape[1]
    member = (iota((heads, lanes), 0) == first_head + iota((heads, lanes), 1) // head_dim).astype(BF16)
    return dot(jnp.concatenate(split(x), axis=1), jnp.concatenate([member, member], axis=0))


INDEX, WHICH, OWN, HELD = range(4)


def start_all(pairs, sems):
    copies = [pltpu.make_async_copy(source, target, sems.at[i]) for i, (source, target) in enumerate(pairs)]
    for copy in copies:
        copy.start()
    return copies


def head_rows(lanes, head_dim):
    return -(-(lanes // head_dim) // 8) * 8


def tiles_of(x):
    return [x[i : i + 1, j : j + 128] for i in range(x.shape[0]) for j in range(0, x.shape[1], 128)]


def notes_rows(tiles, width):
    return -(-tiles // (width // 128) // 16) * 16


def notes(tiles, width):
    per = width // 128
    rows = notes_rows(len(tiles), width)
    tiles = tiles + [jnp.zeros((1, 128), F32)] * (rows * per - len(tiles))
    rows = [jnp.concatenate(tiles[i : i + per], axis=1) for i in range(0, len(tiles), per)]
    return jnp.concatenate(rows, axis=0).astype(BF16)


def read_notes(ref, counts):
    tiles = tiles_of(ref[pl.ds(N, ref.shape[0] - N), :].astype(F32))
    runs = []
    for count in counts:
        runs.append(tiles[:count])
        tiles = tiles[count:]
    return runs


def wide(tiles):
    return jnp.concatenate(tiles, axis=1)


def heads_of(tiles, rows):
    return jnp.concatenate(tiles + [jnp.zeros((1, 128), F32)] * (rows - len(tiles)), axis=0)


def pieces_of(x):
    return [y.astype(F32) for y in split(x)]


def piece_counts(width, heads):
    return [width // 128] * 2 + [heads] * 2


def first_kernel(head_dim, lanes, place, kq_from, values_from, log_decay_from, *refs):
    *pieces, kq, values, log_decay, sems = refs
    copies = start_all([(log_decay_from, log_decay), (kq_from, kq), (values_from, values)], sems)
    copies[0].wait()
    decay = decay_left(log_decay[...])
    copies[1].wait()
    keys = jnp.transpose(kq[:, :N])
    wides = [spread(decay, first_head(place, m, lanes, head_dim), pieces[0].shape[1], head_dim) for m in range(len(pieces))]
    copies[2].wait()
    for m, piece in enumerate(pieces):
        state_piece(place, m, lanes, 0, keys, values, wides[m], [], piece)


def last_kernel(head_dim, lanes, place, kq, values, log_decay, *pieces):
    width = pieces[0].shape[1]
    at = lanes - width
    ld = log_decay[...]
    heads, rows = ld.shape[0], head_rows(lanes, head_dim)
    decay = decay_left(ld)
    growth = split(jnp.exp(cumulative_by_head(ld)))
    query_sums = dot(growth[0], kq[:, N:]) + dot(growth[1], kq[:, N:])
    keys = jnp.transpose(kq[:, :N])
    for m, piece in enumerate(pieces):
        first = first_head(place, m, lanes, head_dim)
        own = iota((rows, heads), 1) == first + iota((rows, heads), 0)
        mine = dot(own.astype(F32), query_sums, precision=HIGHEST)[: lanes // head_dim]
        tiles = [tile for x in pieces_of(mine) for tile in tiles_of(x)]
        broad = spread(decay, first + at // head_dim, width, head_dim)
        state_piece(place, m, lanes, at, keys, values, broad, tiles, piece)


def first_head(place, m, lanes, head_dim):
    return (place[OWN] ^ m) * (lanes // head_dim)


def decay_left(log_decay):
    by_position = cumulative_by_position(log_decay)
    final = by_position[GROUP - 1 :, :]
    return jnp.concatenate([jnp.exp(final - by_position), jnp.broadcast_to(jnp.exp(final), (8, final.shape[1]))], axis=0)


def state_piece(place, m, lanes, at, keys, values, broad, tiles, piece):
    width = piece.shape[1]
    below = notes([tile for x in pieces_of(broad[GROUP : GROUP + 1]) for tile in tiles_of(x)] + tiles, width)
    piece[pl.ds(N, below.shape[0]), :] = below
    start = pl.multiple_of((place[OWN] ^ m) * lanes + at, 128)
    weighted = (values[:, pl.ds(start, width)].astype(F32) * broad[:GROUP]).astype(BF16)
    piece[pl.ds(0, N), :] = dot(keys, weighted).astype(BF16)


def piece_factor(piece):
    high, low = read_notes(piece, [piece.shape[1] // 128] * 2)
    return wide(high) + wide(low)


def piece_queries(piece, head_dim, widths):
    _, _, high, low = read_notes(piece, piece_counts(widths[-1], sum(widths) // head_dim))
    out, at = [], 0
    for width in widths:
        rows, end = head_rows(width, head_dim), at + width // head_dim
        out.append(jnp.concatenate([heads_of(high[at:end], rows), heads_of(low[at:end], rows)], axis=0))
        at = end
    return out


def block_kernel(head_dim, kq, values, log_decay, skip, out, wide_growth, sums):
    ld = log_decay[...]
    by_position = cumulative_by_position(ld)
    by_head = cumulative_by_head(ld)
    scores = dot(kq[:, N:], kq[:, :N], ((1,), (1,)))
    causal = iota((GROUP, GROUP), 0) >= iota((GROUP, GROUP), 1)
    per = 128 // head_dim
    lane = iota((GROUP, 128), 1) // head_dim
    lane_row = iota((1, 128), 1) // head_dim
    tiles = values.shape[1] // 128
    part_tiles = tiles // (sums.shape[0] // 8)
    sums[...] = jnp.zeros_like(sums)
    for i in range(tiles):
        at = slice(i * 128, (i + 1) * 128)
        value = values[:, at]
        mixes, tops = [], []
        direct = jnp.zeros((1, 128), F32)
        growth = None
        for j in range(per):
            h = i * per + j
            here = jnp.broadcast_to(by_position[:, h : h + 1], (GROUP, 128))
            gap = here - by_head[h : h + 1, :]
            mixes.append((scores * jnp.exp(jnp.where(causal, gap, -jnp.inf))).astype(BF16))
            tops.append(jnp.where(lane == j, value, jnp.zeros_like(value)))
            direct = jnp.where(lane_row == j, skip[h], direct)
            growth = here if growth is None else jnp.where(lane == j, here, growth)
        mixed = dot(jnp.concatenate(mixes, axis=1), jnp.concatenate(tops, axis=0))
        mixed = mixed + direct * value.astype(F32)
        out[:, at] = mixed
        wide_growth[:, at] = jnp.exp(growth)
        line = i // part_tiles * 8 + i % part_tiles
        sums[line : line + 1, :] = jnp.sum(mixed, axis=0, keepdims=True)


def at_index(place, count, body):
    for index in range(count):
        pl.when(place[INDEX] == index)(functools.partial(body, index))


def total_kernel(head_dim, place, *refs):
    *pieces, total = refs
    factors = [piece_factor(piece) for piece in pieces]

    def body(index):
        running = pieces[index][pl.ds(0, N), :].astype(F32)
        for j in range(1, len(pieces)):
            running = factors[j ^ index] * running + pieces[j ^ index][pl.ds(0, N), :].astype(F32)
        total[...] = running.astype(BF16)

    at_index(place, len(pieces), body)


def totals_kernel(head_dim, count, pair, place, sums, *refs):
    scratch = refs[-3 * PIECES :]
    parts, outs = refs[: PIECES * count], refs[PIECES * count : -3 * PIECES]
    lanes = 0
    carried, weights, totals, decays = [], [], [], []
    widths = [scratch[3 * k].shape[2] for k in range(PIECES)]
    for m, piece in enumerate(parts[-count:]):
        for k, x in enumerate(piece_queries(piece, head_dim, widths)):
            scratch[3 * k + 2][place[INDEX] ^ m] = x
    for k in range(PIECES):
        ordered, factors, queries = scratch[3 * k : 3 * k + 3]
        for m, piece in enumerate(parts[k * count : (k + 1) * count]):
            ordered[place[INDEX] ^ m] = piece[pl.ds(0, N), :]
            factors[place[INDEX] ^ m] = piece_factor(piece)
        width = ordered.shape[2]
        lanes += width
        rows = head_rows(width, head_dim)
        running = ordered[0].astype(F32)
        factor = factors[0]
        if pair:
            own = (iota((rows, width), 0) == iota((rows, width), 1) // head_dim).astype(F32) / head_dim
            weight = queries[0, pl.ds(0, rows), :] + queries[0, pl.ds(rows, rows), :]
            added = jnp.zeros((rows, width), F32)
        for j in range(1, count):
            if pair:
                by_head = jnp.sum(own * factor, axis=1, keepdims=True)
                weight = weight + by_head * (queries[j, pl.ds(0, rows), :] + queries[j, pl.ds(rows, rows), :])
                added = added + heads_dot(queries[j].astype(BF16), running.astype(BF16))
            factor = factor * factors[j]
            running = factors[j] * running + ordered[j].astype(F32)
        totals.append(running.astype(BF16))
        decays.append(factor)
        if pair:
            carried.append(own_heads(added, head_dim))
            weights += [tile for x in pieces_of(weight[: width // head_dim]) for tile in tiles_of(x)]
    if not pair:
        for out, x in zip(outs, [*totals, wide(decays)]):
            out[...] = x
        return
    known = wide(sums_tiles(sums[...], lanes)) + in_own_part(place, count, wide(carried))
    below = notes(weights + sums_notes(known), outs[0].shape[1])
    outs[0][pl.ds(0, N), :] = totals[-1]
    outs[0][pl.ds(N, below.shape[0]), :] = below


def sums_tiles(sums, lanes):
    return [sums[i : i + 1] for i in range(sums.shape[0]) if i % 8 < lanes // 128]


def in_own_part(place, count, x):
    return wide([jnp.where(place[OWN] == k, x, 0.0) for k in range(count)])


def starts_kernel(head_dim, count, lanes, place, *refs):
    refs, pieces, outs = refs[: -2 * count], refs[-2 * count : -count], refs[-count:]
    factors = [piece_factor(piece) for piece in pieces]

    def body(index):
        running = jnp.where(place[WHICH] == 0, 0.0, refs[-1][pl.ds(0, N), :].astype(F32))
        for j in range(count):
            outs[j ^ index][pl.ds(0, N), :] = running.astype(BF16)
            if j < count - 1:
                running = factors[j ^ index] * running + pieces[j ^ index][pl.ds(0, N), :].astype(F32)

    at_index(place, count, body)
    if len(refs) > 1:
        sums = sums_of(place, head_dim, lanes, count, refs[: len(refs) // 2], refs[len(refs) // 2 :])
        below = notes(sums_notes(sums), outs[0].shape[1])
        for out in outs:
            out[pl.ds(N, below.shape[0]), :] = below


def sums_notes(sums):
    return [tile for x in pieces_of(sums) for tile in tiles_of(x)]


def sums_of(place, head_dim, lanes, count, totals, before):
    first = place[WHICH] == 0
    counts = []
    for total in totals:
        counts += [total.shape[1] // head_dim] * 2
    counts += [count * lanes // 128] * 2
    mine, other = read_notes(totals[-1], counts), read_notes(before[-1], counts)
    products = []
    for k, (total, got) in enumerate(zip(totals, before)):
        rows = head_rows(total.shape[1], head_dim)
        weight = [
            jnp.where(first, heads_of(there, rows), heads_of(here, rows))
            for here, there in zip(mine[2 * k : 2 * k + 2], other[2 * k : 2 * k + 2])
        ]
        state = jnp.where(first, total[pl.ds(0, N), :].astype(F32), got[pl.ds(0, N), :].astype(F32)).astype(BF16)
        products.append(own_heads(heads_dot(jnp.concatenate(weight, axis=0).astype(BF16), state), head_dim))
    known = sum(wide(here) + wide(there) for here, there in zip(mine[-2:], other[-2:]))
    return known + in_own_part(place, count, wide(products))


def heads_dot(queries, state):
    both = dot(queries, state)
    rows = queries.shape[0] // 2
    return both[:rows] + both[rows:]


def own_heads(x, head_dim):
    mine = iota(x.shape, 0) == iota(x.shape, 1) // head_dim
    return jnp.sum(jnp.where(mine, x, 0.0), axis=0, keepdims=True)


def sums_kernel(head_dim, count, *refs):
    *refs, out = refs
    pieces, states = refs[: PIECES * count], refs[PIECES * count :]
    carried = []
    widths = [pieces[k * count].shape[1] for k in range(PIECES)]
    queries = [piece_queries(piece, head_dim, widths) for piece in pieces[-count:]]
    for k in range(PIECES):
        added = 0.0
        for query, state in zip(queries, states[k * count : (k + 1) * count]):
            added = added + heads_dot(query[k].astype(BF16), state[pl.ds(0, N), :])
        carried.append(own_heads(added, head_dim))
    out[...] = wide(carried)


def output_kernel(ms, count, lanes, offset, step, positions, place, kq, local, wide_growth, *refs):
    carried, refs = refs[: len(ms)], refs[len(ms) :]
    *refs, made, sems = refs
    copies = []
    at = [pl.multiple_of((place[OWN] ^ m) * lanes + offset, 128) for m in ms]
    width = carried[0].shape[1]
    mixed = refs[{0: -1, 1: -3, 2: -4}[step]]
    for i, state in enumerate(carried):
        here = pl.ds(at[i], width)
        made[i] = (local[:, here] + wide_growth[:, here] * dot(kq[:, N:], state[pl.ds(0, N), :])).astype(BF16)
        copies.append(pltpu.make_async_copy(made.at[i], mixed.at[:, here], sems.at[i]))
        copies[-1].start()
    if step == 1:
        weights, (pooled, rows) = refs[:count], refs[-2:]
        for k in range(count):
            rows[place[HELD] ^ place[OWN] ^ k] = weights[k][...]
        pooled[...] = jnp.zeros_like(pooled)
    if step == 2:
        before, rows, logits, pooled, scaled = refs[0], refs[1], refs[-3], refs[-2], refs[-1]
        pooled[...] = before[...]
    if step:
        for m, state in zip(ms, carried):
            high, low = read_notes(state, [count * lanes // 128] * 2)
            for k in range(count):
                part = slice(k * (lanes // 128), (k + 1) * (lanes // 128))
                pooled[place[OWN] ^ k] += jnp.broadcast_to(wide(high[part]) + wide(low[part]), (8, lanes))
    if step == 2:
        product = square = 0.0
        for m in range(count):
            mean = pooled[m] / positions
            high, low = split(mean)
            product = product + dot(high, rows[m]) + dot(low, rows[m])
            square = square + jnp.sum(mean * mean, axis=1, keepdims=True)
        scaled[...] = product / jnp.sqrt(square / (lanes * count) + epsilon)
        copies.append(pltpu.make_async_copy(scaled.at[pl.ds(0, 1)], logits, sems.at[len(ms)]))
        copies[-1].start()
    for copy in copies:
        copy.wait()


def call(kernel, outs, in_specs, scratch=(), flops=0, moved=0, out_specs=None, aliases=None):
    return pl.pallas_call(
        kernel,
        out_shape=outs,
        in_specs=in_specs,
        out_specs=out_specs or jax.tree.map(lambda _: VMEM, outs),
        scratch_shapes=scratch,
        input_output_aliases=aliases or {},
        cost_estimate=pl.CostEstimate(flops=flops, bytes_accessed=moved, transcendentals=0),
        compiler_params=pltpu.CompilerParams(vmem_limit_bytes=LIMIT),
    )


def local(inputs, keys_queries, log_decay, skip, classifier):
    _, positions, channels = inputs.shape
    heads = log_decay.shape[1]
    head_dim = channels // heads
    size, group = lax.axis_size("seq"), lax.axis_size("fsdp")
    pair = size == 2 * group
    lanes = channels // group
    classes = classifier.shape[1]
    index, column = lax.axis_index("seq"), lax.axis_index("fsdp")
    place = jnp.stack([index % group, index // group, (index % group) ^ column, column]).astype(jnp.int32)
    values, kq, ld = inputs[0], keys_queries[0], log_decay[0]
    sources = [pltpu.with_memory_space_constraint(x, pltpu.HBM) for x in (kq, values, ld)]
    landing = [jax.ShapeDtypeStruct(x.shape, x.dtype) for x in (kq, values, ld)]
    tiles = lanes // 128
    widths = [(tiles + 1) // 2 * 128, tiles // 2 * 128] if PIECES == 2 else [lanes]
    offsets = [0, widths[0]][:PIECES]

    def piece(width, count):
        return jax.ShapeDtypeStruct((N + (notes_rows(count, width) if count else 0), width), BF16)

    row = jax.ShapeDtypeStruct((1, lanes), F32)
    full = jax.ShapeDtypeStruct((positions, channels), F32)
    share = jax.ShapeDtypeStruct((8, classes), F32)
    gathered = [
        jax.ShapeDtypeStruct((group, 8, lanes), F32),
        jax.ShapeDtypeStruct((group, lanes, classes), BF16),
    ]
    def swap(x, m, axis="seq"):
        return lax.ppermute(x, axis, [(i, i ^ m) for i in range(lax.axis_size(axis))])

    def swap_all(xs, axis="seq"):
        return [xs[0]] + [swap(xs[m], m, axis) for m in range(1, group)]

    def shift(x, by):
        return lax.ppermute(x, "seq", [(i, i + by) for i in range(size - by)])

    *first, kq, values, ld = call(
        functools.partial(first_kernel, head_dim, lanes),
        [piece(widths[0], sum(piece_counts(widths[0], 0)))] * group + landing,
        [SMEM] + [ANY] * 3,
        [pltpu.SemaphoreType.DMA((3,))],
        flops=2 * positions * N * channels,
        moved=4 * positions * channels,
    )(place, *sources)
    last = call(
        functools.partial(last_kernel, head_dim, lanes),
        [piece(widths[1], sum(piece_counts(widths[1], lanes // head_dim)))] * group,
        [SMEM] + [VMEM] * 3,
    )(place, kq, values, ld)
    parts = [swap_all(first), swap_all(last)]
    classifier, parts[0][1] = lax.optimization_barrier((classifier, parts[0][1]))
    totals = []
    if pair and PIECES == 2:
        totals.append(
            call(
                functools.partial(total_kernel, head_dim),
                piece(widths[0], 0),
                [SMEM] + [VMEM] * group,
            )(place, *parts[0])
        )
        skip = lax.optimization_barrier((skip, totals))[0]
    made = call(
        functools.partial(block_kernel, head_dim),
        [full, full, jax.ShapeDtypeStruct((8 * group, 128), F32)],
        [VMEM] * 3 + [SMEM],
        flops=8 * positions * N * channels,
        moved=6 * positions * channels,
    )(kq, values, ld, skip)
    from_block, wide_growth, sums = made
    scratch = []
    for width in widths:
        scratch += [
            pltpu.VMEM((group, N, width), BF16),
            pltpu.VMEM((group, 1, width), F32),
            pltpu.VMEM((group, 2 * head_rows(width, head_dim), N), F32),
        ]
    totals += call(
        functools.partial(totals_kernel, head_dim, group, pair),
        [piece(widths[-1], 2 * (lanes // head_dim) + 2 * group * tiles)] if pair else [piece(w, 0) for w in widths] + [row],
        [SMEM] + [VMEM] * (1 + PIECES * group),
        scratch,
    )(place, sums, *[x for part in parts for x in part])
    crossed = swap(classifier, 2, "fsdp")
    if pair:
        before = [swap(total, group) for total in totals]
        across = [*totals, *before]
    else:
        *totals, decay = totals
        before = []
        for total, at, width in zip(totals, offsets, widths):
            running, factor = shift(total, group).astype(F32), shift(decay[:, at : at + width], group)
            reach = 1
            while reach < size // group - 1:
                running = running + factor * shift(running, group * reach)
                factor = factor * shift(factor, group * reach)
                reach *= 2
            before.append(running.astype(BF16))

    weights = [classifier, swap(classifier, 1, "fsdp"), crossed, swap(crossed, 1, "fsdp")]
    starts = []
    for k, width in enumerate(widths):
        last = k == PIECES - 1
        operands = across if last and pair else [before[k]]
        starts.append(
            call(
                functools.partial(starts_kernel, head_dim, group, lanes),
                [piece(width, 2 * group * tiles if last and pair else 0)] * group,
                [SMEM] + [VMEM] * (len(operands) + group),
            )(place, *operands, *parts[k])
        )
    if not pair:
        whole = call(
            functools.partial(sums_kernel, head_dim, group), row, [VMEM] * (2 * PIECES * group)
        )(*[x for part in parts for x in part], *[x for part in starts for x in part])
        reach = group
        while reach < size:
            whole = whole + swap(whole, reach)
            reach *= 2
        reach = 1
        while reach < size:
            sums = sums + swap(sums, reach)
            reach *= 2
        known = wide(sums_tiles(sums / group, lanes)) + in_own_part(place, group, whole)
        below = notes(sums_notes(known), widths[-1])
        starts[-1] = [jnp.concatenate([x, below], axis=0) for x in starts[-1]]
    starts = [swap_all(x) for x in starts]

    plan = [(tuple(range(group)), k, 0) for k in range(PIECES - 1)]
    plan += [(tuple(range(group - 1)), PIECES - 1, 1), ((group - 1,), PIECES - 1, 2)]
    mixed, rest = None, []
    for i, (ms, k, step) in enumerate(plan):
        operands = [kq, from_block, wide_growth, *[starts[k][m] for m in ms]]
        operands += {0: [], 1: weights, 2: rest}[step]
        outs = [pltpu.HBM((positions, channels), BF16)]
        outs += {0: [], 1: gathered, 2: [pltpu.HBM((1, classes), F32)]}[step]
        scratch = [pltpu.VMEM(gathered[0].shape, F32), pltpu.VMEM(share.shape, F32)] if step == 2 else []
        mixed, *rest = call(
            functools.partial(output_kernel, ms, group, lanes, offsets[k], step, positions * size),
            outs,
            [SMEM] + [VMEM] * len(operands) + [ANY] * (i > 0),
            scratch
            + [
                pltpu.VMEM((len(ms), positions, widths[k]), BF16),
                pltpu.SemaphoreType.DMA((len(ms) + 1,)),
            ],
            out_specs=[ANY] + {0: [], 1: [VMEM] * 2, 2: [ANY]}[step],
            aliases={1 + len(operands): 0} if i else None,
        )(place, *operands, *([mixed] if i else []))
    (logits,) = rest
    return mixed[None], logits


def solution(mesh):
    return jax.shard_map(
        local,
        mesh=mesh,
        in_specs=(
            P("fsdp", "seq", None),
            P("fsdp", "seq", None),
            P("fsdp", None, "seq"),
            P(),
            P("fsdp", None),
        ),
        out_specs=(P("fsdp", "seq", None), P("fsdp", None)),
        check_vma=False,
    )
```

```python
import functools
import jax
import jax.numpy as jnp
from jax import lax
from jax.experimental import pallas as pl
from jax.experimental.pallas import tpu as pltpu
from jax.sharding import PartitionSpec as P

N = 128
GROUP = 128

epsilon = 1e-06
PIECES = 2

F32 = jnp.float32
BF16 = jnp.bfloat16
HIGHEST = lax.Precision.HIGHEST
LIMIT = 48 * 1024 * 1024

VMEM = pl.BlockSpec(memory_space=pltpu.VMEM)
ANY = pl.BlockSpec(memory_space=pl.ANY)
SMEM = pl.BlockSpec(memory_space=pltpu.SMEM)


def dot(a, b, contract=((1,), (0,)), precision=None):
    return lax.dot_general(a, b, (contract, ((), ())), preferred_element_type=F32, precision=precision)


def iota(shape, dim):
    return lax.broadcasted_iota(jnp.int32, shape, dim)


def split(x):
    high = x.astype(BF16)
    return high, (x - high.astype(F32)).astype(BF16)


def cumulative_by_position(log_decay):
    upto = (iota((GROUP, GROUP), 1) <= iota((GROUP, GROUP), 0)).astype(BF16)
    high = log_decay.astype(BF16)
    middle, low = split(log_decay - high.astype(F32))
    return sum(dot(upto, x, ((1,), (1,))) for x in (low, middle, high))


def cumulative_by_head(log_decay):
    upto = (iota((GROUP, GROUP), 0) <= iota((GROUP, GROUP), 1)).astype(F32)
    return dot(log_decay, upto, precision=HIGHEST)


def spread(x, first_head, lanes, head_dim):
    heads = x.shape[1]
    member = (iota((heads, lanes), 0) == first_head + iota((heads, lanes), 1) // head_dim).astype(BF16)
    return dot(jnp.concatenate(split(x), axis=1), jnp.concatenate([member, member], axis=0))


INDEX, WHICH, OWN, HELD = range(4)


def start_all(pairs, sems):
    copies = [pltpu.make_async_copy(source, target, sems.at[i]) for i, (source, target) in enumerate(pairs)]
    for copy in copies:
        copy.start()
    return copies


def head_rows(lanes, head_dim):
    return -(-(lanes // head_dim) // 8) * 8


def tiles_of(x):
    return [x[i : i + 1, j : j + 128] for i in range(x.shape[0]) for j in range(0, x.shape[1], 128)]


def notes_rows(tiles, width):
    return -(-tiles // (width // 128) // 8) * 8


def notes(tiles, width):
    per = width // 128
    rows = notes_rows(len(tiles), width)
    tiles = tiles + [jnp.zeros((1, 128), F32)] * (rows * per - len(tiles))
    rows = [jnp.concatenate(tiles[i : i + per], axis=1) for i in range(0, len(tiles), per)]
    return jnp.concatenate(rows, axis=0).astype(BF16)


def read_notes(ref, counts):
    tiles = tiles_of(ref[pl.ds(N, ref.shape[0] - N), :].astype(F32))
    runs = []
    for count in counts:
        runs.append(tiles[:count])
        tiles = tiles[count:]
    return runs


def wide(tiles):
    return jnp.concatenate(tiles, axis=1)


def heads_of(tiles, rows):
    return jnp.concatenate(tiles + [jnp.zeros((1, 128), F32)] * (rows - len(tiles)), axis=0)


def pieces_of(x):
    return [y.astype(F32) for y in split(x)]


def piece_counts(width, heads):
    return [width // 128] * 2 + [heads] * 2


def first_kernel(head_dim, lanes, place, kq_from, values_from, log_decay_from, *refs):
    *pieces, kq, values, log_decay, sems = refs
    copies = start_all([(log_decay_from, log_decay), (kq_from, kq), (values_from, values)], sems)
    copies[0].wait()
    decay = decay_left(log_decay[...])
    copies[1].wait()
    keys = jnp.transpose(kq[:, :N])
    wides = [spread(decay, first_head(place, m, lanes, head_dim), pieces[0].shape[1], head_dim) for m in range(len(pieces))]
    copies[2].wait()
    for m, piece in enumerate(pieces):
        state_piece(place, m, lanes, 0, keys, values, wides[m], [], piece)


def last_kernel(head_dim, lanes, place, kq, values, log_decay, *pieces):
    width = pieces[0].shape[1]
    at = lanes - width
    ld = log_decay[...]
    heads, rows = ld.shape[0], head_rows(lanes, head_dim)
    decay = decay_left(ld)
    growth = split(jnp.exp(cumulative_by_head(ld)))
    query_sums = dot(growth[0], kq[:, N:]) + dot(growth[1], kq[:, N:])
    keys = jnp.transpose(kq[:, :N])
    for m, piece in enumerate(pieces):
        first = first_head(place, m, lanes, head_dim)
        own = iota((rows, heads), 1) == first + iota((rows, heads), 0)
        mine = dot(own.astype(F32), query_sums, precision=HIGHEST)[: lanes // head_dim]
        tiles = [tile for x in pieces_of(mine) for tile in tiles_of(x)]
        broad = spread(decay, first + at // head_dim, width, head_dim)
        state_piece(place, m, lanes, at, keys, values, broad, tiles, piece)


def first_head(place, m, lanes, head_dim):
    return (place[OWN] ^ m) * (lanes // head_dim)


def decay_left(log_decay):
    by_position = cumulative_by_position(log_decay)
    final = by_position[GROUP - 1 :, :]
    return jnp.concatenate([jnp.exp(final - by_position), jnp.broadcast_to(jnp.exp(final), (8, final.shape[1]))], axis=0)


def state_piece(place, m, lanes, at, keys, values, broad, tiles, piece):
    width = piece.shape[1]
    below = notes([tile for x in pieces_of(broad[GROUP : GROUP + 1]) for tile in tiles_of(x)] + tiles, width)
    piece[pl.ds(N, below.shape[0]), :] = below
    start = pl.multiple_of((place[OWN] ^ m) * lanes + at, 128)
    weighted = (values[:, pl.ds(start, width)].astype(F32) * broad[:GROUP]).astype(BF16)
    piece[pl.ds(0, N), :] = dot(keys, weighted).astype(BF16)


def piece_factor(piece):
    high, low = read_notes(piece, [piece.shape[1] // 128] * 2)
    return wide(high) + wide(low)


def piece_queries(piece, head_dim, widths):
    _, _, high, low = read_notes(piece, piece_counts(widths[-1], sum(widths) // head_dim))
    out, at = [], 0
    for width in widths:
        rows, end = head_rows(width, head_dim), at + width // head_dim
        out.append(jnp.concatenate([heads_of(high[at:end], rows), heads_of(low[at:end], rows)], axis=0))
        at = end
    return out


def block_kernel(head_dim, kq, values, log_decay, skip, out, wide_growth, sums):
    ld = log_decay[...]
    by_position = cumulative_by_position(ld)
    by_head = cumulative_by_head(ld)
    scores = dot(kq[:, N:], kq[:, :N], ((1,), (1,)))
    causal = iota((GROUP, GROUP), 0) >= iota((GROUP, GROUP), 1)
    per = 128 // head_dim
    lane = iota((GROUP, 128), 1) // head_dim
    lane_row = iota((1, 128), 1) // head_dim
    tiles = values.shape[1] // 128
    part_tiles = tiles // (sums.shape[0] // 8)
    sums[...] = jnp.zeros_like(sums)
    for i in range(tiles):
        at = slice(i * 128, (i + 1) * 128)
        value = values[:, at]
        mixes, tops = [], []
        direct = jnp.zeros((1, 128), F32)
        growth = None
        for j in range(per):
            h = i * per + j
            here = jnp.broadcast_to(by_position[:, h : h + 1], (GROUP, 128))
            gap = here - by_head[h : h + 1, :]
            mixes.append((scores * jnp.exp(jnp.where(causal, gap, -jnp.inf))).astype(BF16))
            tops.append(jnp.where(lane == j, value, jnp.zeros_like(value)))
            direct = jnp.where(lane_row == j, skip[h], direct)
            growth = here if growth is None else jnp.where(lane == j, here, growth)
        mixed = dot(jnp.concatenate(mixes, axis=1), jnp.concatenate(tops, axis=0))
        mixed = mixed + direct * value.astype(F32)
        out[:, at] = mixed
        wide_growth[:, at] = jnp.exp(growth)
        line = i // part_tiles * 8 + i % part_tiles
        sums[line : line + 1, :] = jnp.sum(mixed, axis=0, keepdims=True)


def at_index(place, count, body):
    for index in range(count):
        pl.when(place[INDEX] == index)(functools.partial(body, index))


def total_kernel(head_dim, place, *refs):
    *pieces, total = refs
    factors = [piece_factor(piece) for piece in pieces]

    def body(index):
        running = pieces[index][pl.ds(0, N), :].astype(F32)
        for j in range(1, len(pieces)):
            running = factors[j ^ index] * running + pieces[j ^ index][pl.ds(0, N), :].astype(F32)
        total[...] = running.astype(BF16)

    at_index(place, len(pieces), body)


def totals_kernel(head_dim, count, pair, place, sums, *refs):
    scratch = refs[-3 * PIECES :]
    parts, outs = refs[: PIECES * count], refs[PIECES * count : -3 * PIECES]
    lanes = 0
    carried, weights, totals, decays = [], [], [], []
    widths = [scratch[3 * k].shape[2] for k in range(PIECES)]
    for m, piece in enumerate(parts[-count:]):
        for k, x in enumerate(piece_queries(piece, head_dim, widths)):
            scratch[3 * k + 2][place[INDEX] ^ m] = x
    for k in range(PIECES):
        ordered, factors, queries = scratch[3 * k : 3 * k + 3]
        for m, piece in enumerate(parts[k * count : (k + 1) * count]):
            ordered[place[INDEX] ^ m] = piece[pl.ds(0, N), :]
            factors[place[INDEX] ^ m] = piece_factor(piece)
        width = ordered.shape[2]
        lanes += width
        rows = head_rows(width, head_dim)
        running = ordered[0].astype(F32)
        factor = factors[0]
        if pair:
            own = (iota((rows, width), 0) == iota((rows, width), 1) // head_dim).astype(F32) / head_dim
            weight = queries[0, pl.ds(0, rows), :] + queries[0, pl.ds(rows, rows), :]
            added = jnp.zeros((rows, width), F32)
        for j in range(1, count):
            if pair:
                by_head = jnp.sum(own * factor, axis=1, keepdims=True)
                weight = weight + by_head * (queries[j, pl.ds(0, rows), :] + queries[j, pl.ds(rows, rows), :])
                added = added + heads_dot(queries[j].astype(BF16), running.astype(BF16))
            factor = factor * factors[j]
            running = factors[j] * running + ordered[j].astype(F32)
        totals.append(running.astype(BF16))
        decays.append(factor)
        if pair:
            carried.append(own_heads(added, head_dim))
            weights += [tile for x in pieces_of(weight[: width // head_dim]) for tile in tiles_of(x)]
    if not pair:
        for out, x in zip(outs, [*totals, wide(decays)]):
            out[...] = x
        return
    known = wide(sums_tiles(sums[...], lanes)) + in_own_part(place, count, wide(carried))
    below = notes(weights + sums_notes(known), outs[0].shape[1])
    outs[0][pl.ds(0, N), :] = totals[-1]
    outs[0][pl.ds(N, below.shape[0]), :] = below


def sums_tiles(sums, lanes):
    return [sums[i : i + 1] for i in range(sums.shape[0]) if i % 8 < lanes // 128]


def in_own_part(place, count, x):
    return wide([jnp.where(place[OWN] == k, x, 0.0) for k in range(count)])


def starts_kernel(head_dim, count, lanes, place, *refs):
    refs, pieces, outs = refs[: -2 * count], refs[-2 * count : -count], refs[-count:]
    factors = [piece_factor(piece) for piece in pieces]

    def body(index):
        running = jnp.where(place[WHICH] == 0, 0.0, refs[-1][pl.ds(0, N), :].astype(F32))
        for j in range(count):
            outs[j ^ index][pl.ds(0, N), :] = running.astype(BF16)
            if j < count - 1:
                running = factors[j ^ index] * running + pieces[j ^ index][pl.ds(0, N), :].astype(F32)

    at_index(place, count, body)
    if len(refs) > 1:
        sums = sums_of(place, head_dim, lanes, count, refs[: len(refs) // 2], refs[len(refs) // 2 :])
        below = notes(sums_notes(sums), outs[0].shape[1])
        for out in outs:
            out[pl.ds(N, below.shape[0]), :] = below


def sums_notes(sums):
    return [tile for x in pieces_of(sums) for tile in tiles_of(x)]


def sums_of(place, head_dim, lanes, count, totals, before):
    first = place[WHICH] == 0
    counts = []
    for total in totals:
        counts += [total.shape[1] // head_dim] * 2
    counts += [count * lanes // 128] * 2
    mine, other = read_notes(totals[-1], counts), read_notes(before[-1], counts)
    products = []
    for k, (total, got) in enumerate(zip(totals, before)):
        rows = head_rows(total.shape[1], head_dim)
        weight = [
            jnp.where(first, heads_of(there, rows), heads_of(here, rows))
            for here, there in zip(mine[2 * k : 2 * k + 2], other[2 * k : 2 * k + 2])
        ]
        state = jnp.where(first, total[pl.ds(0, N), :].astype(F32), got[pl.ds(0, N), :].astype(F32)).astype(BF16)
        products.append(own_heads(heads_dot(jnp.concatenate(weight, axis=0).astype(BF16), state), head_dim))
    known = sum(wide(here) + wide(there) for here, there in zip(mine[-2:], other[-2:]))
    return known + in_own_part(place, count, wide(products))


def heads_dot(queries, state):
    both = dot(queries, state)
    rows = queries.shape[0] // 2
    return both[:rows] + both[rows:]


def own_heads(x, head_dim):
    mine = iota(x.shape, 0) == iota(x.shape, 1) // head_dim
    return jnp.sum(jnp.where(mine, x, 0.0), axis=0, keepdims=True)


def sums_kernel(head_dim, count, *refs):
    *refs, out = refs
    pieces, states = refs[: PIECES * count], refs[PIECES * count :]
    carried = []
    widths = [pieces[k * count].shape[1] for k in range(PIECES)]
    queries = [piece_queries(piece, head_dim, widths) for piece in pieces[-count:]]
    for k in range(PIECES):
        added = 0.0
        for query, state in zip(queries, states[k * count : (k + 1) * count]):
            added = added + heads_dot(query[k].astype(BF16), state[pl.ds(0, N), :])
        carried.append(own_heads(added, head_dim))
    out[...] = wide(carried)


def output_kernel(ms, count, lanes, offset, step, positions, place, kq, local, wide_growth, *refs):
    carried, refs = refs[: len(ms)], refs[len(ms) :]
    *refs, made, sems = refs
    copies = []
    at = [pl.multiple_of((place[OWN] ^ m) * lanes + offset, 128) for m in ms]
    width = carried[0].shape[1]
    mixed = refs[{0: -1, 1: -3, 2: -4}[step]]
    for i, state in enumerate(carried):
        here = pl.ds(at[i], width)
        made[i] = (local[:, here] + wide_growth[:, here] * dot(kq[:, N:], state[pl.ds(0, N), :])).astype(BF16)
        copies.append(pltpu.make_async_copy(made.at[i], mixed.at[:, here], sems.at[i]))
        copies[-1].start()
    if step == 1:
        weights, (pooled, rows) = refs[:count], refs[-2:]
        for k in range(count):
            rows[place[HELD] ^ place[OWN] ^ k] = weights[k][...]
        pooled[...] = jnp.zeros_like(pooled)
    if step == 2:
        before, rows, logits, pooled, scaled = refs[0], refs[1], refs[-3], refs[-2], refs[-1]
        pooled[...] = before[...]
    if step:
        for m, state in zip(ms, carried):
            high, low = read_notes(state, [count * lanes // 128] * 2)
            for k in range(count):
                part = slice(k * (lanes // 128), (k + 1) * (lanes // 128))
                pooled[place[OWN] ^ k] += jnp.broadcast_to(wide(high[part]) + wide(low[part]), (8, lanes))
    if step == 2:
        product = square = 0.0
        for m in range(count):
            mean = pooled[m] / positions
            high, low = split(mean)
            product = product + dot(high, rows[m]) + dot(low, rows[m])
            square = square + jnp.sum(mean * mean, axis=1, keepdims=True)
        scaled[...] = product / jnp.sqrt(square / (lanes * count) + epsilon)
        copies.append(pltpu.make_async_copy(scaled.at[pl.ds(0, 1)], logits, sems.at[len(ms)]))
        copies[-1].start()
    for copy in copies:
        copy.wait()


def call(kernel, outs, in_specs, scratch=(), flops=0, moved=0, out_specs=None, aliases=None):
    return pl.pallas_call(
        kernel,
        out_shape=outs,
        in_specs=in_specs,
        out_specs=out_specs or jax.tree.map(lambda _: VMEM, outs),
        scratch_shapes=scratch,
        input_output_aliases=aliases or {},
        cost_estimate=pl.CostEstimate(flops=flops, bytes_accessed=moved, transcendentals=0),
        compiler_params=pltpu.CompilerParams(vmem_limit_bytes=LIMIT),
    )


def local(inputs, keys_queries, log_decay, skip, classifier):
    _, positions, channels = inputs.shape
    heads = log_decay.shape[1]
    head_dim = channels // heads
    size, group = lax.axis_size("seq"), lax.axis_size("fsdp")
    pair = size == 2 * group
    lanes = channels // group
    classes = classifier.shape[1]
    index, column = lax.axis_index("seq"), lax.axis_index("fsdp")
    place = jnp.stack([index % group, index // group, (index % group) ^ column, column]).astype(jnp.int32)
    values, kq, ld = inputs[0], keys_queries[0], log_decay[0]
    sources = [pltpu.with_memory_space_constraint(x, pltpu.HBM) for x in (kq, values, ld)]
    landing = [jax.ShapeDtypeStruct(x.shape, x.dtype) for x in (kq, values, ld)]
    tiles = lanes // 128
    widths = [(tiles + 1) // 2 * 128, tiles // 2 * 128] if PIECES == 2 else [lanes]
    offsets = [0, widths[0]][:PIECES]

    def piece(width, count):
        return jax.ShapeDtypeStruct((N + (notes_rows(count, width) if count else 0), width), BF16)

    row = jax.ShapeDtypeStruct((1, lanes), F32)
    full = jax.ShapeDtypeStruct((positions, channels), F32)
    share = jax.ShapeDtypeStruct((8, classes), F32)
    gathered = [
        jax.ShapeDtypeStruct((group, 8, lanes), F32),
        jax.ShapeDtypeStruct((group, lanes, classes), BF16),
    ]
    def swap(x, m, axis="seq"):
        return lax.ppermute(x, axis, [(i, i ^ m) for i in range(lax.axis_size(axis))])

    def swap_all(xs, axis="seq"):
        return [xs[0]] + [swap(xs[m], m, axis) for m in range(1, group)]

    def shift(x, by):
        return lax.ppermute(x, "seq", [(i, i + by) for i in range(size - by)])

    *first, kq, values, ld = call(
        functools.partial(first_kernel, head_dim, lanes),
        [piece(widths[0], sum(piece_counts(widths[0], 0)))] * group + landing,
        [SMEM] + [ANY] * 3,
        [pltpu.SemaphoreType.DMA((3,))],
        flops=2 * positions * N * channels,
        moved=4 * positions * channels,
    )(place, *sources)
    last = call(
        functools.partial(last_kernel, head_dim, lanes),
        [piece(widths[1], sum(piece_counts(widths[1], lanes // head_dim)))] * group,
        [SMEM] + [VMEM] * 3,
    )(place, kq, values, ld)
    parts = [swap_all(first), swap_all(last)]
    classifier, parts[0][1] = lax.optimization_barrier((classifier, parts[0][1]))
    totals = []
    if pair and PIECES == 2:
        totals.append(
            call(
                functools.partial(total_kernel, head_dim),
                piece(widths[0], 0),
                [SMEM] + [VMEM] * group,
            )(place, *parts[0])
        )
        skip = lax.optimization_barrier((skip, totals))[0]
    made = call(
        functools.partial(block_kernel, head_dim),
        [full, full, jax.ShapeDtypeStruct((8 * group, 128), F32)],
        [VMEM] * 3 + [SMEM],
        flops=8 * positions * N * channels,
        moved=6 * positions * channels,
    )(kq, values, ld, skip)
    from_block, wide_growth, sums = made
    scratch = []
    for width in widths:
        scratch += [
            pltpu.VMEM((group, N, width), BF16),
            pltpu.VMEM((group, 1, width), F32),
            pltpu.VMEM((group, 2 * head_rows(width, head_dim), N), F32),
        ]
    totals += call(
        functools.partial(totals_kernel, head_dim, group, pair),
        [piece(widths[-1], 2 * (lanes // head_dim) + 2 * group * tiles)] if pair else [piece(w, 0) for w in widths] + [row],
        [SMEM] + [VMEM] * (1 + PIECES * group),
        scratch,
    )(place, sums, *[x for part in parts for x in part])
    crossed = swap(classifier, 2, "fsdp")
    if pair:
        before = [swap(total, group) for total in totals]
        across = [*totals, *before]
    else:
        *totals, decay = totals
        before = []
        for total, at, width in zip(totals, offsets, widths):
            running, factor = shift(total, group).astype(F32), shift(decay[:, at : at + width], group)
            reach = 1
            while reach < size // group - 1:
                running = running + factor * shift(running, group * reach)
                factor = factor * shift(factor, group * reach)
                reach *= 2
            before.append(running.astype(BF16))

    weights = [classifier, swap(classifier, 1, "fsdp"), crossed, swap(crossed, 1, "fsdp")]
    starts = []
    for k, width in enumerate(widths):
        last = k == PIECES - 1
        operands = across if last and pair else [before[k]]
        starts.append(
            call(
                functools.partial(starts_kernel, head_dim, group, lanes),
                [piece(width, 2 * group * tiles if last and pair else 0)] * group,
                [SMEM] + [VMEM] * (len(operands) + group),
            )(place, *operands, *parts[k])
        )
    if not pair:
        whole = call(
            functools.partial(sums_kernel, head_dim, group), row, [VMEM] * (2 * PIECES * group)
        )(*[x for part in parts for x in part], *[x for part in starts for x in part])
        reach = group
        while reach < size:
            whole = whole + swap(whole, reach)
            reach *= 2
        reach = 1
        while reach < size:
            sums = sums + swap(sums, reach)
            reach *= 2
        known = wide(sums_tiles(sums / group, lanes)) + in_own_part(place, group, whole)
        below = notes(sums_notes(known), widths[-1])
        starts[-1] = [jnp.concatenate([x, below], axis=0) for x in starts[-1]]
    starts = [swap_all(x) for x in starts]

    plan = [((0, 3, 1, 2), k, 0) for k in range(PIECES - 1)]
    plan += [(tuple(range(group - 1)), PIECES - 1, 1), ((group - 1,), PIECES - 1, 2)]
    mixed, rest = None, []
    for i, (ms, k, step) in enumerate(plan):
        operands = [kq, from_block, wide_growth, *[starts[k][m] for m in ms]]
        operands += {0: [], 1: weights, 2: rest}[step]
        outs = [pltpu.HBM((positions, channels), BF16)]
        outs += {0: [], 1: gathered, 2: [pltpu.HBM((1, classes), F32)]}[step]
        scratch = [pltpu.VMEM(gathered[0].shape, F32), pltpu.VMEM(share.shape, F32)] if step == 2 else []
        mixed, *rest = call(
            functools.partial(output_kernel, ms, group, lanes, offsets[k], step, positions * size),
            outs,
            [SMEM] + [VMEM] * len(operands) + [ANY] * (i > 0),
            scratch
            + [
                pltpu.VMEM((len(ms), positions, widths[k]), BF16),
                pltpu.SemaphoreType.DMA((len(ms) + 1,)),
            ],
            out_specs=[ANY] + {0: [], 1: [VMEM] * 2, 2: [ANY]}[step],
            aliases={1 + len(operands): 0} if i else None,
        )(place, *operands, *([mixed] if i else []))
    (logits,) = rest
    return mixed[None], logits


def solution(mesh):
    return jax.shard_map(
        local,
        mesh=mesh,
        in_specs=(
            P("fsdp", "seq", None),
            P("fsdp", "seq", None),
            P("fsdp", None, "seq"),
            P(),
            P("fsdp", None),
        ),
        out_specs=(P("fsdp", "seq", None), P("fsdp", None)),
        check_vma=False,
    )
```

```python
import functools
import jax
import jax.numpy as jnp
from jax import lax
from jax.experimental import pallas as pl
from jax.experimental.pallas import tpu as pltpu
from jax.sharding import PartitionSpec as P

N = 128
GROUP = 128

epsilon = 1e-06
PIECES = 2

F32 = jnp.float32
BF16 = jnp.bfloat16
HIGHEST = lax.Precision.HIGHEST
LIMIT = 48 * 1024 * 1024

VMEM = pl.BlockSpec(memory_space=pltpu.VMEM)
ANY = pl.BlockSpec(memory_space=pl.ANY)
SMEM = pl.BlockSpec(memory_space=pltpu.SMEM)


def dot(a, b, contract=((1,), (0,)), precision=None):
    return lax.dot_general(a, b, (contract, ((), ())), preferred_element_type=F32, precision=precision)


def iota(shape, dim):
    return lax.broadcasted_iota(jnp.int32, shape, dim)


def split(x):
    high = x.astype(BF16)
    return high, (x - high.astype(F32)).astype(BF16)


def cumulative_by_position(log_decay):
    upto = (iota((GROUP, GROUP), 1) <= iota((GROUP, GROUP), 0)).astype(BF16)
    high = log_decay.astype(BF16)
    middle, low = split(log_decay - high.astype(F32))
    return sum(dot(upto, x, ((1,), (1,))) for x in (low, middle, high))


def cumulative_by_head(log_decay):
    upto = (iota((GROUP, GROUP), 0) <= iota((GROUP, GROUP), 1)).astype(F32)
    return dot(log_decay, upto, precision=HIGHEST)


def spread(x, first_head, lanes, head_dim):
    heads = x.shape[1]
    member = (iota((heads, lanes), 0) == first_head + iota((heads, lanes), 1) // head_dim).astype(BF16)
    return dot(jnp.concatenate(split(x), axis=1), jnp.concatenate([member, member], axis=0))


INDEX, WHICH, OWN, HELD = range(4)


def start_all(pairs, sems):
    copies = [pltpu.make_async_copy(source, target, sems.at[i]) for i, (source, target) in enumerate(pairs)]
    for copy in copies:
        copy.start()
    return copies


def head_rows(lanes, head_dim):
    return -(-(lanes // head_dim) // 8) * 8


def tiles_of(x):
    return [x[i : i + 1, j : j + 128] for i in range(x.shape[0]) for j in range(0, x.shape[1], 128)]


def notes_rows(tiles, width):
    return -(-tiles // (width // 128) // 8) * 8


def notes(tiles, width):
    per = width // 128
    rows = notes_rows(len(tiles), width)
    tiles = tiles + [jnp.zeros((1, 128), F32)] * (rows * per - len(tiles))
    rows = [jnp.concatenate(tiles[i : i + per], axis=1) for i in range(0, len(tiles), per)]
    return jnp.concatenate(rows, axis=0).astype(BF16)


def read_notes(ref, counts):
    tiles = tiles_of(ref[pl.ds(N, ref.shape[0] - N), :].astype(F32))
    runs = []
    for count in counts:
        runs.append(tiles[:count])
        tiles = tiles[count:]
    return runs


def wide(tiles):
    return jnp.concatenate(tiles, axis=1)


def heads_of(tiles, rows):
    return jnp.concatenate(tiles + [jnp.zeros((1, 128), F32)] * (rows - len(tiles)), axis=0)


def pieces_of(x):
    return [y.astype(F32) for y in split(x)]


def piece_counts(width, heads):
    return [width // 128] * 2 + [heads] * 2


def first_kernel(head_dim, lanes, place, kq_from, values_from, log_decay_from, *refs):
    *pieces, kq, values, log_decay, sems = refs
    copies = start_all([(log_decay_from, log_decay), (kq_from, kq), (values_from, values)], sems)
    copies[0].wait()
    decay = decay_left(log_decay[...])
    copies[1].wait()
    keys = jnp.transpose(kq[:, :N])
    wides = [spread(decay, first_head(place, m, lanes, head_dim), pieces[0].shape[1], head_dim) for m in range(len(pieces))]
    copies[2].wait()
    for m, piece in enumerate(pieces):
        state_piece(place, m, lanes, 0, keys, values, wides[m], [], piece)


def last_kernel(head_dim, lanes, place, kq, values, log_decay, *pieces):
    width = pieces[0].shape[1]
    at = lanes - width
    ld = log_decay[...]
    heads, rows = ld.shape[0], head_rows(lanes, head_dim)
    decay = decay_left(ld)
    growth = split(jnp.exp(cumulative_by_head(ld)))
    query_sums = dot(growth[0], kq[:, N:]) + dot(growth[1], kq[:, N:])
    keys = jnp.transpose(kq[:, :N])
    for m, piece in enumerate(pieces):
        first = first_head(place, m, lanes, head_dim)
        own = iota((rows, heads), 1) == first + iota((rows, heads), 0)
        mine = dot(own.astype(F32), query_sums, precision=HIGHEST)[: lanes // head_dim]
        tiles = [tile for x in pieces_of(mine) for tile in tiles_of(x)]
        broad = spread(decay, first + at // head_dim, width, head_dim)
        state_piece(place, m, lanes, at, keys, values, broad, tiles, piece)


def first_head(place, m, lanes, head_dim):
    return (place[OWN] ^ m) * (lanes // head_dim)


def decay_left(log_decay):
    by_position = cumulative_by_position(log_decay)
    final = by_position[GROUP - 1 :, :]
    return jnp.concatenate([jnp.exp(final - by_position), jnp.broadcast_to(jnp.exp(final), (8, final.shape[1]))], axis=0)


def state_piece(place, m, lanes, at, keys, values, broad, tiles, piece):
    width = piece.shape[1]
    below = notes([tile for x in pieces_of(broad[GROUP : GROUP + 1]) for tile in tiles_of(x)] + tiles, width)
    piece[pl.ds(N, below.shape[0]), :] = below
    start = pl.multiple_of((place[OWN] ^ m) * lanes + at, 128)
    weighted = (values[:, pl.ds(start, width)].astype(F32) * broad[:GROUP]).astype(BF16)
    piece[pl.ds(0, N), :] = dot(keys, weighted).astype(BF16)


def piece_factor(piece):
    high, low = read_notes(piece, [piece.shape[1] // 128] * 2)
    return wide(high) + wide(low)


def piece_queries(piece, head_dim, widths):
    _, _, high, low = read_notes(piece, piece_counts(widths[-1], sum(widths) // head_dim))
    out, at = [], 0
    for width in widths:
        rows, end = head_rows(width, head_dim), at + width // head_dim
        out.append(jnp.concatenate([heads_of(high[at:end], rows), heads_of(low[at:end], rows)], axis=0))
        at = end
    return out


def block_kernel(head_dim, kq, values, log_decay, skip, out, wide_growth, sums):
    ld = log_decay[...]
    by_position = cumulative_by_position(ld)
    by_head = cumulative_by_head(ld)
    scores = dot(kq[:, N:], kq[:, :N], ((1,), (1,)))
    causal = iota((GROUP, GROUP), 0) >= iota((GROUP, GROUP), 1)
    per = 128 // head_dim
    lane = iota((GROUP, 128), 1) // head_dim
    lane_row = iota((1, 128), 1) // head_dim
    tiles = values.shape[1] // 128
    part_tiles = tiles // (sums.shape[0] // 8)
    sums[...] = jnp.zeros_like(sums)
    for i in range(tiles):
        at = slice(i * 128, (i + 1) * 128)
        value = values[:, at]
        mixes, tops = [], []
        direct = jnp.zeros((1, 128), F32)
        growth = None
        for j in range(per):
            h = i * per + j
            here = jnp.broadcast_to(by_position[:, h : h + 1], (GROUP, 128))
            gap = here - by_head[h : h + 1, :]
            mixes.append((scores * jnp.exp(jnp.where(causal, gap, -jnp.inf))).astype(BF16))
            tops.append(jnp.where(lane == j, value, jnp.zeros_like(value)))
            direct = jnp.where(lane_row == j, skip[h], direct)
            growth = here if growth is None else jnp.where(lane == j, here, growth)
        mixed = dot(jnp.concatenate(mixes, axis=1), jnp.concatenate(tops, axis=0))
        mixed = mixed + direct * value.astype(F32)
        out[:, at] = mixed
        wide_growth[:, at] = jnp.exp(growth)
        line = i // part_tiles * 8 + i % part_tiles
        sums[line : line + 1, :] = jnp.sum(mixed, axis=0, keepdims=True)


def at_index(place, count, body):
    for index in range(count):
        pl.when(place[INDEX] == index)(functools.partial(body, index))


def total_kernel(head_dim, place, *refs):
    *pieces, total = refs
    factors = [piece_factor(piece) for piece in pieces]

    def body(index):
        running = pieces[index][pl.ds(0, N), :].astype(F32)
        for j in range(1, len(pieces)):
            running = factors[j ^ index] * running + pieces[j ^ index][pl.ds(0, N), :].astype(F32)
        total[...] = running.astype(BF16)

    at_index(place, len(pieces), body)


def totals_kernel(head_dim, count, pair, place, sums, *refs):
    scratch = refs[-3 * PIECES :]
    parts, outs = refs[: PIECES * count], refs[PIECES * count : -3 * PIECES]
    lanes = 0
    carried, weights, totals, decays = [], [], [], []
    widths = [scratch[3 * k].shape[2] for k in range(PIECES)]
    for m, piece in enumerate(parts[-count:]):
        for k, x in enumerate(piece_queries(piece, head_dim, widths)):
            scratch[3 * k + 2][place[INDEX] ^ m] = x
    for k in range(PIECES):
        ordered, factors, queries = scratch[3 * k : 3 * k + 3]
        for m, piece in enumerate(parts[k * count : (k + 1) * count]):
            ordered[place[INDEX] ^ m] = piece[pl.ds(0, N), :]
            factors[place[INDEX] ^ m] = piece_factor(piece)
        width = ordered.shape[2]
        lanes += width
        rows = head_rows(width, head_dim)
        running = ordered[0].astype(F32)
        factor = factors[0]
        if pair:
            own = (iota((rows, width), 0) == iota((rows, width), 1) // head_dim).astype(F32) / head_dim
            weight = queries[0, pl.ds(0, rows), :] + queries[0, pl.ds(rows, rows), :]
            added = jnp.zeros((rows, width), F32)
        for j in range(1, count):
            if pair:
                by_head = jnp.sum(own * factor, axis=1, keepdims=True)
                weight = weight + by_head * (queries[j, pl.ds(0, rows), :] + queries[j, pl.ds(rows, rows), :])
                added = added + heads_dot(queries[j].astype(BF16), running.astype(BF16))
            factor = factor * factors[j]
            running = factors[j] * running + ordered[j].astype(F32)
        totals.append(running.astype(BF16))
        decays.append(factor)
        if pair:
            carried.append(own_heads(added, head_dim))
            weights += [tile for x in pieces_of(weight[: width // head_dim]) for tile in tiles_of(x)]
    if not pair:
        for out, x in zip(outs, [*totals, wide(decays)]):
            out[...] = x
        return
    known = wide(sums_tiles(sums[...], lanes)) + in_own_part(place, count, wide(carried))
    below = notes(weights + sums_notes(known), outs[0].shape[1])
    outs[0][pl.ds(0, N), :] = totals[-1]
    outs[0][pl.ds(N, below.shape[0]), :] = below


def sums_tiles(sums, lanes):
    return [sums[i : i + 1] for i in range(sums.shape[0]) if i % 8 < lanes // 128]


def in_own_part(place, count, x):
    return wide([jnp.where(place[OWN] == k, x, 0.0) for k in range(count)])


def starts_kernel(head_dim, count, lanes, place, *refs):
    refs, pieces, outs = refs[: -2 * count], refs[-2 * count : -count], refs[-count:]
    factors = [piece_factor(piece) for piece in pieces]

    def body(index):
        running = jnp.where(place[WHICH] == 0, 0.0, refs[-1][pl.ds(0, N), :].astype(F32))
        for j in range(count):
            outs[j ^ index][pl.ds(0, N), :] = running.astype(BF16)
            if j < count - 1:
                running = factors[j ^ index] * running + pieces[j ^ index][pl.ds(0, N), :].astype(F32)

    at_index(place, count, body)
    if len(refs) > 1:
        sums = sums_of(place, head_dim, lanes, count, refs[: len(refs) // 2], refs[len(refs) // 2 :])
        below = notes(sums_notes(sums), outs[0].shape[1])
        for out in outs:
            out[pl.ds(N, below.shape[0]), :] = below


def sums_notes(sums):
    return [tile for x in pieces_of(sums) for tile in tiles_of(x)]


def sums_of(place, head_dim, lanes, count, totals, before):
    first = place[WHICH] == 0
    counts = []
    for total in totals:
        counts += [total.shape[1] // head_dim] * 2
    counts += [count * lanes // 128] * 2
    mine, other = read_notes(totals[-1], counts), read_notes(before[-1], counts)
    products = []
    for k, (total, got) in enumerate(zip(totals, before)):
        rows = head_rows(total.shape[1], head_dim)
        weight = [
            jnp.where(first, heads_of(there, rows), heads_of(here, rows))
            for here, there in zip(mine[2 * k : 2 * k + 2], other[2 * k : 2 * k + 2])
        ]
        state = jnp.where(first, total[pl.ds(0, N), :].astype(F32), got[pl.ds(0, N), :].astype(F32)).astype(BF16)
        products.append(own_heads(heads_dot(jnp.concatenate(weight, axis=0).astype(BF16), state), head_dim))
    known = sum(wide(here) + wide(there) for here, there in zip(mine[-2:], other[-2:]))
    return known + in_own_part(place, count, wide(products))


def heads_dot(queries, state):
    both = dot(queries, state)
    rows = queries.shape[0] // 2
    return both[:rows] + both[rows:]


def own_heads(x, head_dim):
    mine = iota(x.shape, 0) == iota(x.shape, 1) // head_dim
    return jnp.sum(jnp.where(mine, x, 0.0), axis=0, keepdims=True)


def sums_kernel(head_dim, count, *refs):
    *refs, out = refs
    pieces, states = refs[: PIECES * count], refs[PIECES * count :]
    carried = []
    widths = [pieces[k * count].shape[1] for k in range(PIECES)]
    queries = [piece_queries(piece, head_dim, widths) for piece in pieces[-count:]]
    for k in range(PIECES):
        added = 0.0
        for query, state in zip(queries, states[k * count : (k + 1) * count]):
            added = added + heads_dot(query[k].astype(BF16), state[pl.ds(0, N), :])
        carried.append(own_heads(added, head_dim))
    out[...] = wide(carried)


def output_kernel(ms, count, lanes, offset, step, positions, place, kq, local, wide_growth, *refs):
    carried, refs = refs[: len(ms)], refs[len(ms) :]
    *refs, made, sems = refs
    copies = []
    at = [pl.multiple_of((place[OWN] ^ m) * lanes + offset, 128) for m in ms]
    width = carried[0].shape[1]
    mixed = refs[{0: -1, 1: -3, 2: -4}[step]]
    for i, state in enumerate(carried):
        here = pl.ds(at[i], width)
        made[i] = (local[:, here] + wide_growth[:, here] * dot(kq[:, N:], state[pl.ds(0, N), :])).astype(BF16)
        copies.append(pltpu.make_async_copy(made.at[i], mixed.at[:, here], sems.at[i]))
        copies[-1].start()
    if step == 1:
        weights, (pooled, rows) = refs[:count], refs[-2:]
        for k in range(count):
            rows[place[HELD] ^ place[OWN] ^ k] = weights[k][...]
        pooled[...] = jnp.zeros_like(pooled)
    if step == 2:
        before, rows, logits, pooled, scaled = refs[0], refs[1], refs[-3], refs[-2], refs[-1]
        pooled[...] = before[...]
    if step:
        for m, state in zip(ms, carried):
            high, low = read_notes(state, [count * lanes // 128] * 2)
            for k in range(count):
                part = slice(k * (lanes // 128), (k + 1) * (lanes // 128))
                pooled[place[OWN] ^ k] += jnp.broadcast_to(wide(high[part]) + wide(low[part]), (8, lanes))
    if step == 2:
        product = square = 0.0
        for m in range(count):
            mean = pooled[m] / positions
            high, low = split(mean)
            product = product + dot(high, rows[m]) + dot(low, rows[m])
            square = square + jnp.sum(mean * mean, axis=1, keepdims=True)
        scaled[...] = product / jnp.sqrt(square / (lanes * count) + epsilon)
        copies.append(pltpu.make_async_copy(scaled.at[pl.ds(0, 1)], logits, sems.at[len(ms)]))
        copies[-1].start()
    for copy in copies:
        copy.wait()


def call(kernel, outs, in_specs, scratch=(), flops=0, moved=0, out_specs=None, aliases=None):
    return pl.pallas_call(
        kernel,
        out_shape=outs,
        in_specs=in_specs,
        out_specs=out_specs or jax.tree.map(lambda _: VMEM, outs),
        scratch_shapes=scratch,
        input_output_aliases=aliases or {},
        cost_estimate=pl.CostEstimate(flops=flops, bytes_accessed=moved, transcendentals=0),
        compiler_params=pltpu.CompilerParams(vmem_limit_bytes=LIMIT),
    )


def local(inputs, keys_queries, log_decay, skip, classifier):
    _, positions, channels = inputs.shape
    heads = log_decay.shape[1]
    head_dim = channels // heads
    size, group = lax.axis_size("seq"), lax.axis_size("fsdp")
    pair = size == 2 * group
    lanes = channels // group
    classes = classifier.shape[1]
    index, column = lax.axis_index("seq"), lax.axis_index("fsdp")
    place = jnp.stack([index % group, index // group, (index % group) ^ column, column]).astype(jnp.int32)
    values, kq, ld = inputs[0], keys_queries[0], log_decay[0]
    sources = [pltpu.with_memory_space_constraint(x, pltpu.HBM) for x in (kq, values, ld)]
    landing = [jax.ShapeDtypeStruct(x.shape, x.dtype) for x in (kq, values, ld)]
    tiles = lanes // 128
    widths = [(tiles + 1) // 2 * 128, tiles // 2 * 128] if PIECES == 2 else [lanes]
    offsets = [0, widths[0]][:PIECES]

    def piece(width, count):
        return jax.ShapeDtypeStruct((N + (notes_rows(count, width) if count else 0), width), BF16)

    row = jax.ShapeDtypeStruct((1, lanes), F32)
    full = jax.ShapeDtypeStruct((positions, channels), F32)
    share = jax.ShapeDtypeStruct((8, classes), F32)
    gathered = [
        jax.ShapeDtypeStruct((group, 8, lanes), F32),
        jax.ShapeDtypeStruct((group, lanes, classes), BF16),
    ]
    def swap(x, m, axis="seq"):
        return lax.ppermute(x, axis, [(i, i ^ m) for i in range(lax.axis_size(axis))])

    def swap_all(xs, axis="seq"):
        return [xs[0]] + [swap(xs[m], m, axis) for m in range(1, group)]

    def shift(x, by):
        return lax.ppermute(x, "seq", [(i, i + by) for i in range(size - by)])

    *first, kq, values, ld = call(
        functools.partial(first_kernel, head_dim, lanes),
        [piece(widths[0], sum(piece_counts(widths[0], 0)))] * group + landing,
        [SMEM] + [ANY] * 3,
        [pltpu.SemaphoreType.DMA((3,))],
        flops=2 * positions * N * channels,
        moved=4 * positions * channels,
    )(place, *sources)
    last = call(
        functools.partial(last_kernel, head_dim, lanes),
        [piece(widths[1], sum(piece_counts(widths[1], lanes // head_dim)))] * group,
        [SMEM] + [VMEM] * 3,
    )(place, kq, values, ld)
    parts = [swap_all(first), swap_all(last)]
    classifier, parts[0][1] = lax.optimization_barrier((classifier, parts[0][1]))
    totals = []
    if pair and PIECES == 2:
        totals.append(
            call(
                functools.partial(total_kernel, head_dim),
                piece(widths[0], 0),
                [SMEM] + [VMEM] * group,
            )(place, *parts[0])
        )
        skip = lax.optimization_barrier((skip, totals))[0]
    made = call(
        functools.partial(block_kernel, head_dim),
        [full, full, jax.ShapeDtypeStruct((8 * group, 128), F32)],
        [VMEM] * 3 + [SMEM],
        flops=8 * positions * N * channels,
        moved=6 * positions * channels,
    )(kq, values, ld, skip)
    from_block, wide_growth, sums = made
    scratch = []
    for width in widths:
        scratch += [
            pltpu.VMEM((group, N, width), BF16),
            pltpu.VMEM((group, 1, width), F32),
            pltpu.VMEM((group, 2 * head_rows(width, head_dim), N), F32),
        ]
    totals += call(
        functools.partial(totals_kernel, head_dim, group, pair),
        [piece(widths[-1], 2 * (lanes // head_dim) + 2 * group * tiles)] if pair else [piece(w, 0) for w in widths] + [row],
        [SMEM] + [VMEM] * (1 + PIECES * group),
        scratch,
    )(place, sums, *[x for part in parts for x in part])
    crossed = swap(classifier, 2, "fsdp")
    if pair:
        before = [swap(total, group) for total in totals]
        across = [*totals, *before]
    else:
        *totals, decay = totals
        before = []
        for total, at, width in zip(totals, offsets, widths):
            running, factor = shift(total, group).astype(F32), shift(decay[:, at : at + width], group)
            reach = 1
            while reach < size // group - 1:
                running = running + factor * shift(running, group * reach)
                factor = factor * shift(factor, group * reach)
                reach *= 2
            before.append(running.astype(BF16))

    starts = []
    for k, width in enumerate(widths):
        last = k == PIECES - 1
        operands = across if last and pair else [before[k]]
        starts.append(
            call(
                functools.partial(starts_kernel, head_dim, group, lanes),
                [piece(width, 2 * group * tiles if last and pair else 0)] * group,
                [SMEM] + [VMEM] * (len(operands) + group),
            )(place, *operands, *parts[k])
        )
        if k == 0:
            classifier, crossed = lax.optimization_barrier((classifier, crossed, starts))[:2]
            weights = [classifier, swap(classifier, 1, "fsdp"), crossed, swap(crossed, 1, "fsdp")]
    if not pair:
        whole = call(
            functools.partial(sums_kernel, head_dim, group), row, [VMEM] * (2 * PIECES * group)
        )(*[x for part in parts for x in part], *[x for part in starts for x in part])
        reach = group
        while reach < size:
            whole = whole + swap(whole, reach)
            reach *= 2
        reach = 1
        while reach < size:
            sums = sums + swap(sums, reach)
            reach *= 2
        known = wide(sums_tiles(sums / group, lanes)) + in_own_part(place, group, whole)
        below = notes(sums_notes(known), widths[-1])
        starts[-1] = [jnp.concatenate([x, below], axis=0) for x in starts[-1]]
    starts = [swap_all(x) for x in starts]

    plan = [((0, 3, 1, 2), k, 0) for k in range(PIECES - 1)]
    plan += [(tuple(range(group - 1)), PIECES - 1, 1), ((group - 1,), PIECES - 1, 2)]
    mixed, rest = None, []
    for i, (ms, k, step) in enumerate(plan):
        operands = [kq, from_block, wide_growth, *[starts[k][m] for m in ms]]
        operands += {0: [], 1: weights, 2: rest}[step]
        outs = [pltpu.HBM((positions, channels), BF16)]
        outs += {0: [], 1: gathered, 2: [pltpu.HBM((1, classes), F32)]}[step]
        scratch = [pltpu.VMEM(gathered[0].shape, F32), pltpu.VMEM(share.shape, F32)] if step == 2 else []
        mixed, *rest = call(
            functools.partial(output_kernel, ms, group, lanes, offsets[k], step, positions * size),
            outs,
            [SMEM] + [VMEM] * len(operands) + [ANY] * (i > 0),
            scratch
            + [
                pltpu.VMEM((len(ms), positions, widths[k]), BF16),
                pltpu.SemaphoreType.DMA((len(ms) + 1,)),
            ],
            out_specs=[ANY] + {0: [], 1: [VMEM] * 2, 2: [ANY]}[step],
            aliases={1 + len(operands): 0} if i else None,
        )(place, *operands, *([mixed] if i else []))
    (logits,) = rest
    return mixed[None], logits


def solution(mesh):
    return jax.shard_map(
        local,
        mesh=mesh,
        in_specs=(
            P("fsdp", "seq", None),
            P("fsdp", "seq", None),
            P("fsdp", None, "seq"),
            P(),
            P("fsdp", None),
        ),
        out_specs=(P("fsdp", "seq", None), P("fsdp", None)),
        check_vma=False,
    )
```
